256 devices in a mesh: wide: 64 (over x, z, y_lo), kv: 4 (over y_hi, core).
Axes of the slice: x: 4, y: 4 (y_hi: 2, y_lo: 2; y = y_hi * 2 + y_lo), z: 8, core: 2. Of those that a mesh axis runs over, the one named last changes fastest.
Arguments:
- prompt_q: bfloat16 [4096, 8192], P('wide', 'kv'), may hold values from -2 to 2
- prompt_k: bfloat16 [4096, 512], P('wide', 'kv'), may hold values from -2 to 2
- prompt_v: bfloat16 [4096, 512], P('wide', 'kv'), may hold values from -6 to 6
- prompt_out: bfloat16 [4096, 8192], P('wide', 'kv'), may hold values from -6 to 6
- prompt_dout: bfloat16 [4096, 8192], P('wide', 'kv'), may hold values from -6 to 6
- resp_q: bfloat16 [4096, 8192], P('wide', 'kv'), may hold values from -2 to 2
- resp_k: bfloat16 [4096, 512], P('wide', 'kv'), may hold values from -2 to 2
- resp_v: bfloat16 [4096, 512], P('wide', 'kv'), may hold values from -6 to 6
- resp_out: bfloat16 [4096, 8192], P('wide', 'kv'), may hold values from -6 to 6
- resp_dout: bfloat16 [4096, 8192], P(('wide', 'kv')), may hold values from -6 to 6
- resp_len: int32 [64], P('wide'), may hold values from 1 to 64, 2560 in all
- loss_mask: int32 [4096], P('wide'), may hold values 0 or 1
Outputs:
- prompt_dq: float32 [4096, 8192], P('wide', 'kv')
- prompt_dk: float32 [4096, 512], P('wide', 'kv')
- prompt_dv: float32 [4096, 512], P('wide', 'kv')
- resp_dq: float32 [4096, 8192], P('wide', 'kv')
- resp_dk: float32 [4096, 512], P('wide', 'kv')
- resp_dv: float32 [4096, 512], P('wide', 'kv')
The draws below stay inside these ranges and needn't reach their ends.
Inputs may be any that keep to these rules, and one draw needn't show every extreme that they name: Response m has resp_len[m] real tokens; slots from resp_len[m] on are padding; the longest response has exactly 64 tokens.
All inputs are finite; a program needn't handle non-finite values. No bound on the sum of `resp_len` or of `loss_mask` on one device may be relied on, other than what follows from the above.
Results may differ from the reference program's by a relative error of at most 0.0029.
Values may be sent and summed in bfloat16 or wider, within the bound.
A program may use at most 64 MiB of HBM per device.

```python
import math
import jax
import jax.numpy as jnp
import numpy as np
from jax import lax

Q_HEADS = 64
KV_HEADS = 4
D_HEAD = 128
RESP = 64
GROUP = 16
PROMPT = 4096
MEMBERS = 64
N_WIDE = 64


def with_ends(values, own_key, smallest, high):
    extent = values.shape
    place = [jax.random.randint(jax.random.fold_in(own_key, axis), (), 0, extent[axis]) for axis in range(len(extent))]
    values = values.at[tuple(place)].set(smallest)
    longest = extent.index(max(extent))
    place[longest] = (place[longest] + 1) % extent[longest]
    return values.at[tuple(place)].set(high)


def steps_of(rng, shape, cuts, low, high):
    gain = 1.0
    for dim, blocks in cuts:
        heights = jax.random.uniform(jax.random.fold_in(jax.random.fold_in(rng, 6), dim), (blocks,), jnp.float32, low / len(cuts), high / len(cuts))
        gain = gain * jnp.repeat(jnp.exp(heights), shape[dim] // blocks).reshape((-1,) + (1,) * (len(shape) - 1 - dim))
    return gain


def length_profile(count, total, most, lean):
    portions = [(1 << 20) // math.isqrt(rank ** lean) + 1 for rank in range(2, count + 1)]
    rest, counts = total - most - (count - 1), [1] * (count - 1)
    while rest > 0:
        candidates = [i for i in range(count - 1) if counts[i] < most]
        whole, budget = sum([portions[i] for i in candidates]), rest
        for i in candidates:
            more = min(most - counts[i], max(1, budget * portions[i] // whole), rest)
            counts[i] = counts[i] + more
            rest = rest - more
    return np.array([most] + counts)


def uneven(rng, count, total, bound, lean):
    if count == 2:
        one = jax.random.randint(rng, (), max(1, total - bound), min(bound, total - 1) + 1)
        return jnp.stack([one, total - one])
    sizes = jnp.asarray(length_profile(count, total, bound, lean), jnp.int32)
    pairs = (count - 1) // 2
    giver, sink = sizes[1:1 + 2 * pairs:2], sizes[2:2 + 2 * pairs:2]
    room = jnp.minimum(giver - 1, bound - sink)
    passed = jax.random.randint(jax.random.fold_in(rng, 1), (pairs,), 0, 1 << 20) % (room + 1)
    sizes = sizes.at[1:1 + 2 * pairs:2].set(giver - passed).at[2:2 + 2 * pairs:2].set(sink + passed)
    return sizes[jax.random.permutation(jax.random.fold_in(rng, 2), count)]


def centred(stream_key, shape, width, limit, shards=(), kind=jnp.bfloat16):
    values = jax.random.normal(stream_key, shape, jnp.float32) * width
    if len(shards) > 0:
        values = steps_of(stream_key, shape, shards, -0.22, 0.18) * values
    return jnp.clip(values, min=-limit, max=limit).astype(kind)


def setup_inputs(seed: int = 0) -> dict:
    streams_of = jax.random.split(jax.random.key(seed), 13)
    prompt_q = jnp.clip(jax.random.uniform(streams_of[0], (PROMPT, Q_HEADS * D_HEAD), jnp.float32, -2.0, 2.0) * steps_of(streams_of[0], (PROMPT, Q_HEADS * D_HEAD), ((0, 64), (1, 4)), -0.4, 0.0), -2.0, 2.0).astype(jnp.bfloat16)
    prompt_k = jnp.clip(jax.random.uniform(streams_of[1], (PROMPT, KV_HEADS * D_HEAD), jnp.float32, -2.0, 2.0) * steps_of(streams_of[1], (PROMPT, KV_HEADS * D_HEAD), ((0, 64), (1, 4)), -0.4, 0.0), -2.0, 2.0).astype(jnp.bfloat16)
    prompt_v = centred(streams_of[2], (PROMPT, KV_HEADS * D_HEAD), 1.0, 6.0, ((0, 64), (1, 4)))
    prompt_out = centred(streams_of[3], (PROMPT, Q_HEADS * D_HEAD), 1.0, 6.0, ((0, 64), (1, 4)))
    prompt_dout = centred(streams_of[4], (PROMPT, Q_HEADS * D_HEAD), 1.0, 6.0, ((0, 64), (1, 4)))
    resp_q = jnp.clip(jax.random.uniform(streams_of[5], (MEMBERS * RESP, Q_HEADS * D_HEAD), jnp.float32, -2.0, 2.0) * steps_of(streams_of[5], (MEMBERS * RESP, Q_HEADS * D_HEAD), ((0, 64), (1, 4)), -0.4, 0.0), -2.0, 2.0).astype(jnp.bfloat16)
    resp_k = jnp.clip(jax.random.uniform(streams_of[6], (MEMBERS * RESP, KV_HEADS * D_HEAD), jnp.float32, -2.0, 2.0) * steps_of(streams_of[6], (MEMBERS * RESP, KV_HEADS * D_HEAD), ((0, 64), (1, 4)), -0.4, 0.0), -2.0, 2.0).astype(jnp.bfloat16)
    resp_v = centred(streams_of[7], (MEMBERS * RESP, KV_HEADS * D_HEAD), 1.0, 6.0, ((0, 64), (1, 4)))
    resp_out = centred(streams_of[8], (MEMBERS * RESP, Q_HEADS * D_HEAD), 1.0, 6.0, ((0, 64), (1, 4)))
    resp_dout = centred(streams_of[9], (MEMBERS * RESP, Q_HEADS * D_HEAD), 1.0, 6.0, ((0, 256),))
    resp_len = uneven(streams_of[10], MEMBERS, N_WIDE * RESP * 5 // 8, RESP, 1).astype(jnp.int32)
    loss_mask = with_ends((jax.random.randint(streams_of[11], (MEMBERS * RESP,), 0, 8) < 7).astype(jnp.int32), jax.random.fold_in(streams_of[11], 1), 0, 1)
    return dict(prompt_q=prompt_q, prompt_k=prompt_k, prompt_v=prompt_v, prompt_out=prompt_out, prompt_dout=prompt_dout, resp_q=resp_q, resp_k=resp_k, resp_v=resp_v, resp_out=resp_out, resp_dout=resp_dout, resp_len=resp_len, loss_mask=loss_mask)


def single_head(queries, cotangent, forward_out, query_pos, key_rows, value_rows, key_pos):
    score_scale = 1.0 / (D_HEAD ** 0.5)
    scores = jnp.dot(queries, key_rows.T, preferred_element_type=jnp.float32) * score_scale
    seen = key_pos[None, :] <= query_pos[:, None]
    log_norm = jnp.log(jnp.sum(jnp.where(seen, jnp.exp(scores), 0.0), axis=1))
    weights = jnp.where(seen, jnp.exp(scores - log_norm[:, None]), 0.0)
    weight_grad = jnp.dot(cotangent, value_rows.T, preferred_element_type=jnp.float32)
    row_dots = jnp.sum(cotangent.astype(jnp.float32) * forward_out.astype(jnp.float32), axis=1)
    score_grad = (weights * (weight_grad - row_dots[:, None])).astype(jnp.bfloat16)
    query_grad = jnp.dot(score_grad, key_rows, preferred_element_type=jnp.float32) * score_scale
    key_grad = jnp.dot(score_grad.T, queries, preferred_element_type=jnp.float32) * score_scale
    value_grad = jnp.dot(weights.astype(jnp.bfloat16).T, cotangent, preferred_element_type=jnp.float32)
    return query_grad, key_grad, value_grad


def group_grads(queries, cotangent, forward_out, query_pos, key_rows, value_rows, key_pos):
    def one_head(inputs):
        return single_head(inputs[0], inputs[1], inputs[2], query_pos, key_rows, value_rows, key_pos)

    query_grad, key_grad, value_grad = lax.map(one_head, (queries, cotangent, forward_out))
    return query_grad, jnp.sum(key_grad, axis=0), jnp.sum(value_grad, axis=0)


def by_heads(array, row_count):
    return array.reshape(row_count, KV_HEADS, GROUP, D_HEAD).transpose(1, 2, 0, 3)


def by_groups(array, row_count):
    return array.reshape(row_count, KV_HEADS, D_HEAD).transpose(1, 0, 2)


def from_heads(array, row_count):
    return array.transpose(2, 0, 1, 3).reshape(row_count, Q_HEADS * D_HEAD)


def from_groups(array, row_count):
    return array.transpose(1, 0, 2).reshape(row_count, KV_HEADS * D_HEAD)


def reference(prompt_q, prompt_k, prompt_v, prompt_out, prompt_dout, resp_q, resp_k, resp_v, resp_out, resp_dout, resp_len, loss_mask):
    prompt_pos = jnp.arange(PROMPT, dtype=jnp.int32)
    head_queries = by_heads(prompt_q, PROMPT)
    head_cot = by_heads(prompt_dout, PROMPT)
    head_out = by_heads(prompt_out, PROMPT)
    group_keys = by_groups(prompt_k, PROMPT)
    group_values = by_groups(prompt_v, PROMPT)

    def prompt_group(inputs):
        return group_grads(inputs[0], inputs[1], inputs[2], prompt_pos, inputs[3], inputs[4], prompt_pos)

    prompt_query_grad, prompt_key_grad, prompt_value_grad = lax.map(prompt_group, (head_queries, head_cot, head_out, group_keys, group_values))

    resp_pos = PROMPT + jnp.arange(RESP, dtype=jnp.int32)
    all_pos = jnp.concatenate([prompt_pos, resp_pos])
    slot_pos = jnp.arange(RESP, dtype=jnp.int32)

    def member(totals, inputs):
        member_q, member_k, member_v, member_out, member_dout, length, mask_row = inputs
        usable = (slot_pos < length) & (mask_row == 1)
        member_cot = jnp.where(usable[:, None], member_dout, jnp.zeros_like(member_dout))
        keys_all = jnp.concatenate([group_keys, by_groups(member_k, RESP)], axis=1)
        values_all = jnp.concatenate([group_values, by_groups(member_v, RESP)], axis=1)

        def resp_group(parts):
            return group_grads(parts[0], parts[1], parts[2], resp_pos, parts[3], parts[4], all_pos)

        query_grad, key_grad, value_grad = lax.map(resp_group, (by_heads(member_q, RESP), by_heads(member_cot, RESP), by_heads(member_out, RESP), keys_all, values_all))
        new_totals = (totals[0] + key_grad[:, :PROMPT], totals[1] + value_grad[:, :PROMPT])
        return new_totals, (from_heads(query_grad, RESP), from_groups(key_grad[:, PROMPT:], RESP), from_groups(value_grad[:, PROMPT:], RESP))

    member_inputs = (
        resp_q.reshape(MEMBERS, RESP, Q_HEADS * D_HEAD),
        resp_k.reshape(MEMBERS, RESP, KV_HEADS * D_HEAD),
        resp_v.reshape(MEMBERS, RESP, KV_HEADS * D_HEAD),
        resp_out.reshape(MEMBERS, RESP, Q_HEADS * D_HEAD),
        resp_dout.reshape(MEMBERS, RESP, Q_HEADS * D_HEAD),
        resp_len,
        loss_mask.reshape(MEMBERS, RESP),
    )
    (key_total, value_total), (resp_query_grad, resp_key_grad, resp_value_grad) = lax.scan(member, (prompt_key_grad, prompt_value_grad), member_inputs)
    return (
        from_heads(prompt_query_grad, PROMPT),
        from_groups(key_total, PROMPT),
        from_groups(value_total, PROMPT),
        resp_query_grad.reshape(MEMBERS * RESP, Q_HEADS * D_HEAD),
        resp_key_grad.reshape(MEMBERS * RESP, KV_HEADS * D_HEAD),
        resp_value_grad.reshape(MEMBERS * RESP, KV_HEADS * D_HEAD),
    )
```

```python
import functools
import math

import jax
import jax.numpy as jnp
from jax import lax
from jax.experimental import pallas as pl
from jax.experimental.pallas import tpu as pltpu
from jax.sharding import PartitionSpec as P

MESH = pl.DeviceIdType.MESH
BF = jnp.bfloat16
F32 = jnp.float32
NX, NZ, NY = 4, 8, 2
R = 64
D = 128
H = 16
ROWS = H * R
SCALE = 1.0 / math.sqrt(D)
EXP2_SCALE = math.log2(math.e) / math.sqrt(D)
HALF = NX * NZ * R
ABLK = NX * R
BBLK = NZ * R
NN = (((1,), (0,)), ((), ()))
NT = (((1,), (1,)), ((), ()))
TN = (((0,), (0,)), ((), ()))
COPIES = 48
DEFER = 4


def dot(a, b, dims):
    return lax.dot_general(a, b, dims, preferred_element_type=F32)


def by_head(ref):
    return jnp.concatenate([ref[:, h * D : (h + 1) * D] for h in range(H)], axis=0)


def lane_dots(a, b):
    prod = a.astype(F32) * b.astype(F32)
    high = prod.astype(BF)
    low = (prod - high.astype(F32)).astype(BF)
    ones = jnp.ones((8, D), BF)
    return dot(ones, high, NT) + dot(ones, low, NT)


def gray(t):
    return t + (t // 2) * (1 - 2 * lax.rem(t, 2))


def kernel(
    pq, pk, pv, po, pdo, rq, rk, rv, ro, rdo, rlen, lmask,
    pdq, pdk, pdv, rdq, rdk, rdv,
    kvb, qs, dos, arrived, e, eo, dss, zs, dvec, dqt, part, acc_a, acc_b,
    s_r, s_l, r_r, r_l, sb_r, sb_l, rb_r, rb_l, xa_r, zb_s, zb_r, tot, yr,
    ssem, rsem,
):
    w, kv = lax.axis_index("wide"), lax.axis_index("kv")
    x, z, y = w // (NZ * NY), lax.rem(w // NY, NZ), lax.rem(w, NY)

    def dev(xx, zz, yy, vv):
        return ((xx * NZ + zz) * NY + yy, vv)

    def xp(i):
        return dev(lax.rem(x + i, NX), z, y, kv)

    def zp(i):
        return dev(x, lax.rem(z + i, NZ), y, kv)

    yp = dev(x, z, 1 - y, kv)

    def vp(i):
        return dev(x, z, y, lax.rem(kv + i, 4))

    barrier = pltpu.get_barrier_semaphore()
    peers = [yp] + [xp(i) for i in range(1, NX)] + [zp(i) for i in range(1, NZ)] + [vp(i) for i in range(1, 4)]
    for peer in peers:
        pl.semaphore_signal(barrier, inc=1, device_id=peer, device_id_type=MESH)

    sem_no = {}

    def copy(key, src, dst, to):
        i = sem_no.setdefault(key, len(sem_no))
        return pltpu.make_async_remote_copy(
            src_ref=src, dst_ref=dst, send_sem=ssem.at[i], recv_sem=rsem.at[i],
            device_id=to, device_id_type=MESH,
        )

    def off_a(zz):
        return pl.multiple_of(zz * ABLK, ABLK)

    def off_b(xx):
        return pl.multiple_of(HALF + xx * BBLK, BBLK)

    def rows(off, n):
        return kvb.at[pl.ds(pl.multiple_of(off, R), n)]

    own = (1 - y) * (z * ABLK + x * R) + y * (HALF + x * BBLK + z * R)

    def g_y():
        return copy("gy", rows(own, R), rows(own, R), yp)

    def g_ax(i):
        b = rows(z * ABLK + x * R, R)
        return copy(("gax", i), b, b, xp(i))

    def g_bz(i):
        b = rows(HALF + x * BBLK + z * R, R)
        return copy(("gbz", i), b, b, zp(i))

    def g_zr(right, s):
        zz = lax.rem(z + (NZ - s if right else s), NZ)
        if s < 3:
            b = rows(zz * ABLK, ABLK)
        elif right:
            b = rows(zz * ABLK, ABLK // 2)
        else:
            b = rows(zz * ABLK + ABLK // 2, ABLK // 2)
        return copy(("gzr", right, s), b, b, zp(1 if right else NZ - 1))

    def g_xr(right, s):
        xx = lax.rem(x + (NX - s if right else s), NX)
        if s < 1:
            b = rows(HALF + xx * BBLK, BBLK)
        elif right:
            b = rows(HALF + xx * BBLK, BBLK // 2)
        else:
            b = rows(HALF + xx * BBLK + BBLK // 2, BBLK // 2)
        return copy(("gxr", right, s), b, b, xp(1 if right else NX - 1))

    def g_v(i):
        col = pl.multiple_of(lax.rem(kv + i, 4) * (H * D), H * D)
        return copy(
            ("gv", i),
            rdo.at[:, pl.ds(col, H * D)],
            arrived.at[pl.ds(pl.multiple_of(kv * 16, 16), 16)],
            vp(i),
        )

    def t_zr(right, t):
        if right:
            return copy(("tzr", t), s_r.at[t], r_r.at[t], zp(1))
        return copy(("tzl", t), s_l.at[t], r_l.at[t], zp(NZ - 1))

    def t_xr(right, t):
        if right:
            return copy(("txr", t), sb_r.at[t], rb_r.at[t], xp(1))
        return copy(("txl", t), sb_l, rb_l, xp(NX - 1))

    def t_ax(i):
        src = acc_a.at[pl.ds(pl.multiple_of(lax.rem(x + i, NX) * R, R), R)]
        return copy(("tax", i), src, xa_r.at[i], xp(i))

    def t_bz(i):
        return copy(("tbz", i), zb_s.at[pl.ds(pl.multiple_of(lax.rem(z + i, NZ) * R, R), R)], zb_r.at[i], zp(i))

    def t_y():
        return copy("ty", tot.at[1 - y], yr, yp)

    kvb[pl.ds(pl.multiple_of(own, R), R), 0:D] = pk[...]
    kvb[pl.ds(pl.multiple_of(own, R), R), D : 2 * D] = pv[...]
    qs[0:ROWS] = by_head(pq)
    qs[ROWS : 2 * ROWS] = by_head(rq)
    prompt_cot = by_head(pdo)
    dos[0:ROWS] = prompt_cot
    dvec[:, 0:ROWS] = lane_dots(prompt_cot, by_head(po))
    dqt[...] = jnp.zeros_like(dqt)
    row_minus_col = lax.broadcasted_iota(jnp.int32, (R, ROWS), 0) - lax.rem(
        lax.broadcasted_iota(jnp.int32, (R, ROWS), 1), R
    )
    own_e = jnp.where(
        row_minus_col <= 0, jnp.exp2(dot(rk[...], qs[ROWS : 2 * ROWS], NT) * EXP2_SCALE), 0.0
    )
    eo[...] = own_e
    zs[:, 0:ROWS] = jnp.zeros((8, ROWS), F32)
    zs[:, ROWS : 2 * ROWS] = jnp.sum(own_e.reshape(R // 8, 8, ROWS), axis=0)
    pl.semaphore_wait(barrier, len(peers))

    g_y().start()
    for i in range(1, 4):
        g_v(i).start()
    arrived[pl.ds(pl.multiple_of(kv * 16, 16), 16), :] = rdo[:, pl.ds(pl.multiple_of(kv * (H * D), H * D), H * D)]
    g_y().wait_recv()
    for i in range(1, NX):
        g_ax(i).start()
    for i in (4, 3, 5, 2, 6, 1, 7):
        g_bz(i).start()
    for i in range(1, NX):
        g_ax(i).wait_recv()
    g_zr(True, 0).start()
    g_zr(False, 0).start()

    def first(j, carry):
        t, is_b = j // 2, 1 - lax.rem(j, 2)

        @pl.when(j == 0)
        def _():
            for i in range(1, NZ):
                g_bz(i).wait_recv()
            g_xr(True, 0).start()
            g_xr(False, 0).start()

        for s in range(4):

            @pl.when(j == 2 * s + 1)
            def _():
                g_zr(True, s).wait_recv()
                g_zr(False, s).wait_recv()
                if s < 3:
                    g_zr(True, s + 1).start()
                    g_zr(False, s + 1).start()

        @pl.when(j == 2)
        def _():
            g_xr(True, 0).wait_recv()
            g_xr(False, 0).wait_recv()
            g_xr(True, 1).start()
            g_xr(False, 1).start()

        @pl.when(j == 6)
        def _():
            g_xr(True, 1).wait_recv()
            g_xr(False, 1).wait_recv()

        za, zb = lax.rem(z + NZ - t - 1, NZ), lax.rem(z + lax.rem(t + 1, 4), NZ)
        xb = lax.rem(x + gray(t), NX)
        off1 = is_b * (HALF + xb * BBLK) + (1 - is_b) * (za * ABLK)
        off2 = is_b * (HALF + xb * BBLK + BBLK // 2) + (1 - is_b) * (zb * ABLK)
        stride = is_b * (NY * R) + (1 - is_b) * (NZ * NY * R)
        base1 = is_b * (xb * (NZ * NY * R) + R) + (1 - is_b) * (za * (NY * R))
        base2 = is_b * (xb * (NZ * NY * R) + (NZ // 2) * NY * R + R) + (1 - is_b) * (zb * (NY * R))
        off1, off2 = pl.multiple_of(off1, 256), pl.multiple_of(off2, 256)
        keys = jnp.concatenate([kvb[pl.ds(off1, 256), 0:D], kvb[pl.ds(off2, 256), 0:D]], axis=0)
        ex = jnp.exp2(dot(keys, qs[...], NT) * EXP2_SCALE)
        seen = []
        for g in range(8):
            limit = w * R - (base1 if g < 4 else base2) - (g % 4) * stride
            seen.append(jnp.where(row_minus_col <= limit, ex[g * R : (g + 1) * R, 0:ROWS], 0.0))
        seen = jnp.concatenate(seen, axis=0)
        rest = ex[:, ROWS : 2 * ROWS]
        for k, off in ((0, off1), (1, off2)):
            e[pl.ds(off, 256), 0:ROWS] = seen[k * 256 : (k + 1) * 256]
            e[pl.ds(off, 256), ROWS : 2 * ROWS] = rest[k * 256 : (k + 1) * 256]
        zs[:, 0:ROWS] += jnp.sum(seen.reshape(64, 8, ROWS), axis=0)
        zs[:, ROWS : 2 * ROWS] += jnp.sum(rest.reshape(64, 8, ROWS), axis=0)
        return carry

    lax.fori_loop(0, 8, first, 0)

    for i in range(1, 4):
        g_v(i).wait_recv()
    tokens = lax.broadcasted_iota(jnp.int32, (R, R), 1)
    usable = (lmask[...] == 1) & (lax.broadcasted_iota(jnp.int32, (1, R), 1) < rlen[0])
    diagonal = lax.broadcasted_iota(jnp.int32, (R, R), 0) == tokens
    keep = jnp.sum(jnp.where(diagonal & usable, 1.0, 0.0), axis=1, keepdims=True)
    keep = jnp.broadcast_to(keep, (R, D)) > 0.5
    keep = jnp.concatenate([keep] * H, axis=0)
    cot = jnp.where(keep, by_head(arrived).astype(F32), 0.0).astype(BF)
    dos[ROWS : 2 * ROWS] = cot
    dvec[:, ROWS : 2 * ROWS] = lane_dots(cot, by_head(ro))
    zs[...] = jnp.broadcast_to(1.0 / jnp.sum(zs[...], axis=0, keepdims=True), zs.shape)

    def second(j, carry):
        t, is_a = j // 2, 1 - lax.rem(j, 2)
        xb = lax.rem(x + gray(3 - t), NX)
        off1 = is_a * (lax.rem(z + 4 - t, NZ) * ABLK) + (1 - is_a) * (HALF + xb * BBLK)
        off2 = is_a * (lax.rem(z + 5 + t, NZ) * ABLK) + (1 - is_a) * (HALF + xb * BBLK + BBLK // 2)
        off1, off2 = pl.multiple_of(off1, 256), pl.multiple_of(off2, 256)
        pair = jnp.concatenate([kvb[pl.ds(off1, 256), :], kvb[pl.ds(off2, 256), :]], axis=0)
        keys, values = pair[:, 0:D], pair[:, D : 2 * D]
        ex = jnp.concatenate([e[pl.ds(off1, 256), :], e[pl.ds(off2, 256), :]], axis=0)
        weights = ex * zs[0:1, :]
        part[:, D : 2 * D] = dot(weights.astype(BF), dos[...], NN)
        weight_grad = dot(values, dos[...], NT)
        score_grad = (weights * (weight_grad - dvec[0:1, :])).astype(BF)
        part[:, 0:D] = dot(score_grad, qs[...], NN)

        @pl.when(j < 8 - DEFER)
        def _():
            dqt[...] += dot(keys, score_grad, TN)

        @pl.when(j >= 8 - DEFER)
        def _():
            dss[pl.ds(pl.multiple_of((j - (8 - DEFER)) * 512, 512), 512), :] = score_grad

        for s in range(4):

            @pl.when(j == 2 * s)
            def _():
                right, left = part[0:256, :], part[256:512, :]
                if s > 0:
                    t_zr(True, s - 1).wait_recv()
                    t_zr(False, s - 1).wait_recv()
                    right = right + r_r[s - 1].astype(F32)
                    left = left + r_l[s - 1].astype(F32)
                s_r[s] = right.astype(BF)
                t_zr(True, s).start()
                if s < 3:
                    s_l[s] = left.astype(BF)
                    t_zr(False, s).start()
                else:
                    acc_a[...] = left

        @pl.when(j == 1)
        def _():
            sb_r[0] = part[...].astype(BF)
            t_xr(True, 0).start()

        @pl.when(j == 3)
        def _():
            sb_l[...] = part[...].astype(BF)
            t_xr(False, 0).start()

        @pl.when(j == 5)
        def _():
            t_xr(True, 0).wait_recv()
            sb_r[1] = (part[...] + rb_r[0].astype(F32)).astype(BF)
            t_xr(True, 1).start()

        @pl.when(j == 7)
        def _():
            t_xr(True, 1).wait_recv()
            t_xr(False, 0).wait_recv()
            acc = part[...] + rb_r[1].astype(F32) + rb_l[...].astype(F32)
            acc_b[...] = acc
            zb_s[...] = acc.astype(BF)
            for i in (4, 3, 5, 2, 6, 1, 7):
                t_bz(i).start()

        return carry

    lax.fori_loop(0, 8, second, 0)

    def late(i, carry):
        j = i + (8 - DEFER)
        t, is_a = j // 2, 1 - lax.rem(j, 2)
        xb = lax.rem(x + gray(3 - t), NX)
        off1 = is_a * (lax.rem(z + 4 - t, NZ) * ABLK) + (1 - is_a) * (HALF + xb * BBLK)
        off2 = is_a * (lax.rem(z + 5 + t, NZ) * ABLK) + (1 - is_a) * (HALF + xb * BBLK + BBLK // 2)
        off1, off2 = pl.multiple_of(off1, 256), pl.multiple_of(off2, 256)
        keys = jnp.concatenate([kvb[pl.ds(off1, 256), 0:D], kvb[pl.ds(off2, 256), 0:D]], axis=0)
        dqt[...] += dot(keys, dss[pl.ds(pl.multiple_of(i * 512, 512), 512), :], TN)

        @pl.when(i == DEFER // 2 - 1)
        def _():
            t_zr(True, 3).wait_recv()
            acc_a[...] += r_r[3].astype(F32)
            for k in range(1, NX):
                t_ax(k).start()

        return carry

    lax.fori_loop(0, DEFER, late, 0)

    own_w = eo[...] * zs[0:1, ROWS : 2 * ROWS]
    rdv[...] = dot(own_w.astype(BF), dos[ROWS : 2 * ROWS], NN)
    own_g = dot(rv[...], dos[ROWS : 2 * ROWS], NT) - dvec[0:1, ROWS : 2 * ROWS]
    own_g = (own_w * own_g).astype(BF)
    rdk[...] = dot(own_g, qs[ROWS : 2 * ROWS], NN) * SCALE
    dqt[:, ROWS : 2 * ROWS] += dot(rk[...], own_g, TN)

    for i in range(1, NX):
        t_ax(i).wait_recv()
    total = acc_a[pl.ds(pl.multiple_of(x * R, R), R), :]
    for i in range(1, NX):
        total = total + xa_r[i]
    tot[0] = total
    for i in range(1, NZ):
        t_bz(i).wait_recv()
    total = acc_b[pl.ds(pl.multiple_of(z * R, R), R), :]
    for i in range(1, NZ):
        total = total + zb_r[i].astype(F32)
    tot[1] = total
    t_y().start()
    for h in range(0, H, 2):
        for out, first_col in ((pdq, 0), (rdq, ROWS)):
            block = dqt[:, first_col + h * R : first_col + (h + 2) * R].T * SCALE
            out[:, h * D : (h + 1) * D] = block[0:R]
            out[:, (h + 1) * D : (h + 2) * D] = block[R : 2 * R]
    t_y().wait_recv()
    final = tot[y] + yr[...]
    pdk[...] = final[:, 0:D] * SCALE
    pdv[...] = final[:, D : 2 * D]

    g_y().wait_send()
    t_y().wait_send()
    for i in range(1, NX):
        g_ax(i).wait_send()
        t_ax(i).wait_send()
    for i in range(1, NZ):
        g_bz(i).wait_send()
        t_bz(i).wait_send()
    for i in range(1, 4):
        g_v(i).wait_send()
    for s in range(4):
        g_zr(True, s).wait_send()
        g_zr(False, s).wait_send()
        t_zr(True, s).wait_send()
        if s < 3:
            t_zr(False, s).wait_send()
    for s in range(2):
        g_xr(True, s).wait_send()
        g_xr(False, s).wait_send()
        t_xr(True, s).wait_send()
    t_xr(False, 0).wait_send()


def local(
    prompt_q, prompt_k, prompt_v, prompt_out, prompt_dout,
    resp_q, resp_k, resp_v, resp_out, resp_dout, resp_len, loss_mask,
):
    vmem = pl.BlockSpec(memory_space=pltpu.VMEM)
    smem = pl.BlockSpec(memory_space=pltpu.SMEM)
    wide_out = jax.ShapeDtypeStruct((R, H * D), F32)
    head_out = jax.ShapeDtypeStruct((R, D), F32)
    V = pltpu.VMEM
    return pl.pallas_call(
        kernel,
        out_shape=[wide_out, head_out, head_out, wide_out, head_out, head_out],
        in_specs=[vmem] * 10 + [smem, vmem],
        out_specs=[vmem] * 6,
        scratch_shapes=[
            V((2 * HALF, 2 * D), BF),
            V((2 * ROWS, D), BF),
            V((2 * ROWS, D), BF),
            V((R, H * D), BF),
            V((2 * HALF, 2 * ROWS), F32),
            V((R, ROWS), F32),
            V((DEFER * 512, 2 * ROWS), BF),
            V((8, 2 * ROWS), F32),
            V((8, 2 * ROWS), F32),
            V((D, 2 * ROWS), F32),
            V((512, 2 * D), F32),
            V((ABLK, 2 * D), F32),
            V((BBLK, 2 * D), F32),
            V((4, ABLK, 2 * D), BF),
            V((3, ABLK, 2 * D), BF),
            V((4, ABLK, 2 * D), BF),
            V((3, ABLK, 2 * D), BF),
            V((2, BBLK, 2 * D), BF),
            V((BBLK, 2 * D), BF),
            V((2, BBLK, 2 * D), BF),
            V((BBLK, 2 * D), BF),
            V((NX, R, 2 * D), F32),
            V((BBLK, 2 * D), BF),
            V((NZ, R, 2 * D), BF),
            V((2, R, 2 * D), F32),
            V((R, 2 * D), F32),
            pltpu.SemaphoreType.DMA((COPIES,)),
            pltpu.SemaphoreType.DMA((COPIES,)),
        ],
        compiler_params=pltpu.CompilerParams(
            collective_id=0, has_side_effects=True, vmem_limit_bytes=62 * 2**20
        ),
    )(
        prompt_q, prompt_k, prompt_v, prompt_out, prompt_dout,
        resp_q, resp_k, resp_v, resp_out, resp_dout, resp_len, loss_mask.reshape(1, R),
    )


def solution(mesh):
    grid = P("wide", "kv")
    return jax.shard_map(
        local,
        mesh=mesh,
        in_specs=(grid,) * 9 + (P(("wide", "kv"), None), P("wide"), P("wide")),
        out_specs=(grid,) * 6,
        check_vma=False,
    )
```

```python
import functools
import math

import jax
import jax.numpy as jnp
from jax import lax
from jax.experimental import pallas as pl
from jax.experimental.pallas import tpu as pltpu
from jax.sharding import PartitionSpec as P

MESH = pl.DeviceIdType.MESH
BF = jnp.bfloat16
F32 = jnp.float32
NX, NZ, NY = 4, 8, 2
NU = NX * NY
R = 64
S = R // 2
D = 128
H = 16
ROWS = H * R
SCALE = 1.0 / math.sqrt(D)
EXP2_SCALE = math.log2(math.e) / math.sqrt(D)
HALF = NU * NZ * S
BLK = NU * S
SUBS = 4
PIECE = BLK // SUBS
SUMS = 2
SUM_PIECE = BLK // SUMS
NN = (((1,), (0,)), ((), ()))
NT = (((1,), (1,)), ((), ()))
TN = (((0,), (0,)), ((), ()))
COPIES = 87
EARLY = 2


def dot(a, b, dims):
    return lax.dot_general(a, b, dims, preferred_element_type=F32)


def by_head(ref):
    return jnp.concatenate([ref[:, h * D : (h + 1) * D] for h in range(H)], axis=0)


def lane_dots(a, b):
    prod = a.astype(F32) * b.astype(F32)
    high = prod.astype(BF)
    low = (prod - high.astype(F32)).astype(BF)
    ones = jnp.ones((8, D), BF)
    return dot(ones, high, NT) + dot(ones, low, NT)


def kernel(
    pq_hbm, pk_hbm, pv_hbm, po_hbm, pdo_hbm, rq_hbm, rk_hbm, rv_hbm, ro_hbm, rdo_hbm, rlen, lmask,
    dq_hbm, kvg_hbm,
    pq, pk, pv, po, pdo, rq, rk, rv, ro, rdo, dq, kvg,
    kvb, qs, dos, arrived, e, eo, dss, zs, dvec, dqt, part, acc_p, acc_q,
    s_r, s_l, r_r, r_l, sq, rq_in, sp_out, rp_in, sz_out, rz_in,
    ssem, rsem, lsem, osem,
):
    w, kv = lax.axis_index("wide"), lax.axis_index("kv")
    x, z, y = w // (NZ * NY), lax.rem(w // NY, NZ), lax.rem(w, NY)
    u = x * NY + y

    def dev(uu, zz, vv):
        return (((uu // NY) * NZ + zz) * NY + lax.rem(uu, NY), vv)

    def up(i):
        return dev(lax.rem(u + i, NU), z, kv)

    def zp(i):
        return dev(u, lax.rem(z + i, NZ), kv)

    def vp(i):
        return dev(u, z, lax.rem(kv + i, 4))

    barrier = pltpu.get_barrier_semaphore()
    peers = [zp(i) for i in range(1, NZ)] + [up(i) for i in range(1, NU)] + [vp(i) for i in range(1, 4)]
    for peer in peers:
        pl.semaphore_signal(barrier, inc=1, device_id=peer, device_id_type=MESH)

    hbm = (pk_hbm, pv_hbm, rq_hbm, rk_hbm, pq_hbm, pdo_hbm, po_hbm, rdo_hbm, ro_hbm, rv_hbm)
    loads = [
        pltpu.make_async_copy(src, dst, lsem.at[i])
        for i, (src, dst) in enumerate(zip(hbm, (pk, pv, rq, rk, pq, pdo, po, rdo, ro, rv), strict=True))
    ]
    for load in loads:
        load.start()

    sem_no = {}

    def copy(key, src, dst, to):
        i = sem_no.setdefault(key, len(sem_no))
        return pltpu.make_async_remote_copy(
            src_ref=src, dst_ref=dst, send_sem=ssem.at[i], recv_sem=rsem.at[i],
            device_id=to, device_id_type=MESH,
        )

    def rows(off, n):
        return kvb.at[pl.ds(pl.multiple_of(off, S), n)]

    own_p = z * BLK + u * S
    own_q = HALF + u * BLK + z * S

    def g_pu(i):
        return copy(("gpu", i), rows(own_p, S), rows(own_p, S), up(i))

    def g_qz(i):
        return copy(("gqz", i), rows(own_q, S), rows(own_q, S), zp(i))

    def g_pz(right, s, k):
        b = rows(lax.rem(z + (NZ - s if right else s), NZ) * BLK + k * PIECE, PIECE)
        return copy(("gpz", right, s, k), b, b, zp(1 if right else NZ - 1))

    def g_qu(i):
        return copy(("gqu", i), rows(HALF + u * BLK, BLK), rows(HALF + u * BLK, BLK), up(i))

    def g_v(i):
        col = pl.multiple_of(lax.rem(kv + i, 4) * (H * D), H * D)
        return copy(
            ("gv", i),
            rdo.at[:, pl.ds(col, H * D)],
            arrived.at[pl.ds(pl.multiple_of(kv * 16, 16), 16)],
            vp(i),
        )

    def pieces(right, s):
        if s < NZ // 2 - 1:
            return range(SUBS)
        return range(SUBS // 2) if right else range(SUBS // 2, SUBS)

    def t_pz(right, t, k):
        part_of = pl.ds(k * SUM_PIECE, SUM_PIECE)
        if right:
            return copy(("tpr", t, k), s_r.at[t, part_of], r_r.at[t, part_of], zp(1))
        return copy(("tpl", t, k), s_l.at[t, part_of], r_l.at[t, part_of], zp(NZ - 1))

    def t_qu(i):
        return copy(("tqu", i), sq.at[i], rq_in.at[i], up(i))

    def t_pu(i):
        src = sp_out.at[pl.ds(pl.multiple_of(lax.rem(u + i, NU) * S, S), S)]
        return copy(("tpu", i), src, rp_in.at[i], up(i))

    def t_qz(i):
        src = sz_out.at[pl.ds(pl.multiple_of(lax.rem(z + i, NZ) * S, S), S)]
        return copy(("tqz", i), src, rz_in.at[i], zp(i))

    for load in loads:
        load.wait()
    for off, first_row in ((own_p, 0), (own_q, S)):
        kvb[pl.ds(pl.multiple_of(off, S), S), 0:D] = pk[first_row : first_row + S, :]
        kvb[pl.ds(pl.multiple_of(off, S), S), D : 2 * D] = pv[first_row : first_row + S, :]
    qs[0:ROWS] = by_head(pq)
    qs[ROWS : 2 * ROWS] = by_head(rq)
    prompt_cot = by_head(pdo)
    dos[0:ROWS] = prompt_cot
    dvec[:, 0:ROWS] = lane_dots(prompt_cot, by_head(po))
    dqt[...] = jnp.zeros_like(dqt)
    row_minus_col = lax.broadcasted_iota(jnp.int32, (R, ROWS), 0) - lax.rem(
        lax.broadcasted_iota(jnp.int32, (R, ROWS), 1), R
    )
    own_e = jnp.where(
        row_minus_col <= 0, jnp.exp2(dot(rk[...], qs[ROWS : 2 * ROWS], NT) * EXP2_SCALE), 0.0
    )
    eo[...] = own_e
    zs[:, 0:ROWS] = jnp.zeros((8, ROWS), F32)
    zs[:, ROWS : 2 * ROWS] = jnp.sum(own_e.reshape(R // 8, 8, ROWS), axis=0)
    pl.semaphore_wait(barrier, len(peers))

    for i in range(1, NU):
        g_pu(i).start()
    for i in (4, 3, 5, 2, 6, 1, 7):
        g_qz(i).start()
    for i in range(1, 4):
        g_v(i).start()
    arrived[pl.ds(pl.multiple_of(kv * 16, 16), 16), :] = rdo[:, pl.ds(pl.multiple_of(kv * (H * D), H * D), H * D)]
    for i in range(1, NU):
        g_pu(i).wait_recv()
    for k in range(SUBS):
        g_pz(True, 0, k).start()
        g_pz(False, 0, k).start()
    for i in range(1, NZ):
        g_qz(i).wait_recv()
    for i in range(1, NU):
        g_qu(i).start()

    def response_cotangents():
        for i in range(1, 4):
            g_v(i).wait_recv()
        tokens = lax.broadcasted_iota(jnp.int32, (R, R), 1)
        usable = (lmask[...] == 1) & (lax.broadcasted_iota(jnp.int32, (1, R), 1) < rlen[0])
        diagonal = lax.broadcasted_iota(jnp.int32, (R, R), 0) == tokens
        keep = jnp.sum(jnp.where(diagonal & usable, 1.0, 0.0), axis=1, keepdims=True)
        keep = jnp.broadcast_to(keep, (R, D)) > 0.5
        keep = jnp.concatenate([keep] * H, axis=0)
        cot = jnp.where(keep, by_head(arrived).astype(F32), 0.0).astype(BF)
        dos[ROWS : 2 * ROWS] = cot
        dvec[:, ROWS : 2 * ROWS] = lane_dots(cot, by_head(ro))

    def first(j, carry):
        for s in range(NZ // 2):

            @pl.when(j == (s + 1 if s < NZ // 2 - 1 else 7))
            def _():
                for k in range(SUBS):
                    for right in (True, False):
                        if k in pieces(right, s):
                            g_pz(right, s, k).wait_recv()
                            if s < NZ // 2 - 1 and k in pieces(right, s + 1):
                                g_pz(right, s + 1, k).start()
                if s == NZ // 2 - 1:
                    g_qu(NU - 1).wait_recv()

        @pl.when(j == NU // 2)
        def _():
            response_cotangents()

        for c in range(1, NU // 2):

            @pl.when(j == NU // 2 - 1 + c)
            def _():
                g_qu(2 * c - 1).wait_recv()
                g_qu(2 * c).wait_recv()

        q, opening, closing = j // 4, 1 - (j + 7) // 8, j // 7
        p1, p2 = 1 - q + closing, (1 - q) * (1 - opening)
        z1 = lax.rem(z + NZ - j * (1 - q) - 4 * closing, NZ)
        z2 = lax.rem(z + j, NZ)
        u1 = lax.rem(u + 2 * NU + 7 - 2 * j, NU)
        u2 = lax.rem(u + 2 * NU - q * (2 * j - 6) + closing, NU)
        off1 = p1 * (z1 * BLK) + (1 - p1) * (HALF + u1 * BLK)
        off2 = p2 * (z2 * BLK) + (1 - p2) * (HALF + u2 * BLK)
        off1, off2 = pl.multiple_of(off1, BLK), pl.multiple_of(off2, BLK)
        keys = jnp.concatenate([kvb[pl.ds(off1, 256), 0:D], kvb[pl.ds(off2, 256), 0:D]], axis=0)
        ex = jnp.exp2(dot(keys, qs[...], NT) * EXP2_SCALE)
        seen = []
        for p, zz, uu, top in ((p1, z1, u1, 0), (p2, z2, u2, BLK)):
            for g in range(8):
                in_p = (g // NY) * (NZ * NY) + zz * NY + g % NY
                in_q = (uu // NY) * (NZ * NY) + g * NY + lax.rem(uu, NY)
                limit = (w - (p * in_p + (1 - p) * in_q)) * R - (1 - p) * S
                block = ex[top + g * S : top + (g + 1) * S, 0:ROWS]
                seen.append(jnp.where(row_minus_col[0:S] <= limit, block, 0.0))
        seen = jnp.concatenate(seen, axis=0)
        rest = ex[:, ROWS : 2 * ROWS]
        for k, off in ((0, off1), (1, off2)):
            e[pl.ds(off, 256), 0:ROWS] = seen[k * 256 : (k + 1) * 256]
            e[pl.ds(off, 256), ROWS : 2 * ROWS] = rest[k * 256 : (k + 1) * 256]
        zs[:, 0:ROWS] += jnp.sum(seen.reshape(64, 8, ROWS), axis=0)
        zs[:, ROWS : 2 * ROWS] += jnp.sum(rest.reshape(64, 8, ROWS), axis=0)
        return carry

    lax.fori_loop(0, 8, first, 0)

    zs[...] = jnp.broadcast_to(1.0 / jnp.sum(zs[...], axis=0, keepdims=True), zs.shape)

    def chunk(j):
        t, mixed, odd = j // 2, j // 6, lax.rem(j, 2)
        p1, p2 = (1 - mixed) * (1 - odd) + mixed, (1 - mixed) * (1 - odd)
        z1, z2 = lax.rem(z + 4 - t - mixed * odd, NZ), lax.rem(z + 5 + t, NZ)
        u1, u2 = lax.rem(u + 2 * t + 1, NU), lax.rem(u + 2 * t + 2 - mixed * (1 - odd), NU)
        off1 = p1 * (z1 * BLK) + (1 - p1) * (HALF + u1 * BLK)
        off2 = p2 * (z2 * BLK) + (1 - p2) * (HALF + u2 * BLK)
        return pl.multiple_of(off1, BLK), pl.multiple_of(off2, BLK)

    def second(j, carry):
        off1, off2 = chunk(j)
        pair = jnp.concatenate([kvb[pl.ds(off1, 256), :], kvb[pl.ds(off2, 256), :]], axis=0)
        keys, values = pair[:, 0:D], pair[:, D : 2 * D]
        ex = jnp.concatenate([e[pl.ds(off1, 256), :], e[pl.ds(off2, 256), :]], axis=0)
        weights = ex * zs[0:1, :]
        part[:, D : 2 * D] = dot(weights.astype(BF), dos[...], NN)
        weight_grad = dot(values, dos[...], NT)
        score_grad = (weights * (weight_grad - dvec[0:1, :])).astype(BF)
        part[:, 0:D] = dot(score_grad, qs[...], NN)

        @pl.when(j < EARLY)
        def _():
            dqt[...] += dot(keys, score_grad, TN)

        @pl.when(j >= EARLY)
        def _():
            dss[pl.ds(pl.multiple_of((j - EARLY) * 512, 512), 512), :] = score_grad

        for t in range(3):

            @pl.when(j == 2 * t)
            def _():
                for k in range(SUMS):
                    piece = pl.ds(k * SUM_PIECE, SUM_PIECE)
                    right = part[k * SUM_PIECE : (k + 1) * SUM_PIECE, :]
                    left = part[BLK + k * SUM_PIECE : BLK + (k + 1) * SUM_PIECE, :]
                    if t > 0:
                        t_pz(True, t - 1, k).wait_recv()
                        right = right + r_r[t - 1, piece].astype(F32)
                    s_r[t, piece] = right.astype(BF)
                    t_pz(True, t, k).start()
                    if t > 0:
                        t_pz(False, t - 1, k).wait_recv()
                        left = left + r_l[t - 1, piece].astype(F32)
                    s_l[t, piece] = left.astype(BF)
                    t_pz(False, t, k).start()

            @pl.when(j == 2 * t + 1)
            def _():
                sq[2 * t + 1] = part[0:BLK, :].astype(BF)
                t_qu(2 * t + 1).start()
                sq[2 * t + 2] = part[BLK : 2 * BLK, :].astype(BF)
                t_qu(2 * t + 2).start()

        @pl.when(j == 6)
        def _():
            sq[NU - 1] = part[BLK : 2 * BLK, :].astype(BF)
            t_qu(NU - 1).start()
            acc_p[...] = part[0:BLK, :]

        @pl.when(j == 7)
        def _():
            for k in range(SUMS):
                piece = pl.ds(k * SUM_PIECE, SUM_PIECE)
                t_pz(True, 2, k).wait_recv()
                s_r[3, piece] = (acc_p[piece] + r_r[2, piece].astype(F32)).astype(BF)
                t_pz(True, 3, k).start()
            acc_p[...] = part[0:BLK, :]
            acc_q[...] = part[BLK : 2 * BLK, :]

        return carry

    lax.fori_loop(0, 8, second, 0)

    def late(i, carry):
        off1, off2 = chunk(i + EARLY)
        keys = jnp.concatenate([kvb[pl.ds(off1, 256), 0:D], kvb[pl.ds(off2, 256), 0:D]], axis=0)
        dqt[...] += dot(keys, dss[pl.ds(pl.multiple_of(i * 512, 512), 512), :], TN)

        @pl.when(i == 1)
        def _():
            total = acc_q[...]
            for k in range(1, NU):
                t_qu(k).wait_recv()
                total = total + rq_in[k].astype(F32)
            acc_q[...] = total
            sz_out[...] = total.astype(BF)
            for k in (4, 3, 5, 2, 6, 1, 7):
                t_qz(k).start()

        @pl.when(i == 4)
        def _():
            total = acc_p[...]
            for k in range(SUMS):
                t_pz(True, 3, k).wait_recv()
                t_pz(False, 2, k).wait_recv()
            total = total + r_r[3].astype(F32) + r_l[2].astype(F32)
            acc_p[...] = total
            sp_out[...] = total.astype(BF)
            for k in range(1, NU):
                t_pu(k).start()

        return carry

    lax.fori_loop(0, 8 - EARLY, late, 0)

    own_w = eo[...] * zs[0:1, ROWS : 2 * ROWS]
    kvg[3] = dot(own_w.astype(BF), dos[ROWS : 2 * ROWS], NN)
    own_g = dot(rv[...], dos[ROWS : 2 * ROWS], NT) - dvec[0:1, ROWS : 2 * ROWS]
    own_g = (own_w * own_g).astype(BF)
    kvg[2] = dot(own_g, qs[ROWS : 2 * ROWS], NN) * SCALE
    dqt[:, ROWS : 2 * ROWS] += dot(rk[...], own_g, TN)

    stores = [
        pltpu.make_async_copy(dq.at[0], dq_hbm.at[0], osem.at[0]),
        pltpu.make_async_copy(dq.at[1], dq_hbm.at[1], osem.at[1]),
        pltpu.make_async_copy(kvg, kvg_hbm, osem.at[2]),
    ]
    for which, first_col in ((0, 0), (1, ROWS)):
        for h in range(0, H, 2):
            block = dqt[:, first_col + h * R : first_col + (h + 2) * R].T * SCALE
            dq[which, :, h * D : (h + 1) * D] = block[0:R]
            dq[which, :, (h + 1) * D : (h + 2) * D] = block[R : 2 * R]
        stores[which].start()

    for i in range(1, NU):
        t_qz(i).wait_recv()
        t_pu(i).wait_recv()
    for acc, arrivals, place, first_row in ((acc_p, rp_in, u, 0), (acc_q, rz_in, z, S)):
        total = acc[pl.ds(pl.multiple_of(place * S, S), S), :]
        for i in range(1, NU):
            total = total + arrivals[i].astype(F32)
        kvg[0, first_row : first_row + S, :] = total[:, 0:D] * SCALE
        kvg[1, first_row : first_row + S, :] = total[:, D : 2 * D]
    stores[2].start()

    for i in range(1, NU):
        for sent in (g_pu, g_qz, g_qu, t_qu, t_pu, t_qz):
            sent(i).wait_send()
    for i in range(1, 4):
        g_v(i).wait_send()
    for right in (True, False):
        for s in range(NZ // 2):
            for k in pieces(right, s):
                g_pz(right, s, k).wait_send()
            if right or s < 3:
                for k in range(SUMS):
                    t_pz(right, s, k).wait_send()
    for store in stores:
        store.wait()


def hand_out(dq, kvg, pdq, pdk, pdv, rdq, rdk, rdv):
    pdq[...] = dq[0]
    rdq[...] = dq[1]
    for i, out in enumerate((pdk, pdv, rdk, rdv)):
        out[...] = kvg[i]


def local(
    prompt_q, prompt_k, prompt_v, prompt_out, prompt_dout,
    resp_q, resp_k, resp_v, resp_out, resp_dout, resp_len, loss_mask,
):
    vmem = pl.BlockSpec(memory_space=pltpu.VMEM)
    smem = pl.BlockSpec(memory_space=pltpu.SMEM)
    anywhere = pl.BlockSpec(memory_space=pl.ANY)
    wide_out = jax.ShapeDtypeStruct((R, H * D), F32)
    head_out = jax.ShapeDtypeStruct((R, D), F32)
    V = pltpu.VMEM
    wide_in, head_in = V((R, H * D), BF), V((R, D), BF)
    sums = pl.pallas_call(
        kernel,
        out_shape=[jax.ShapeDtypeStruct((2, R, H * D), F32), jax.ShapeDtypeStruct((4, R, D), F32)],
        in_specs=[anywhere] * 10 + [smem, vmem],
        out_specs=[anywhere] * 2,
        scratch_shapes=[
            wide_in, head_in, head_in, wide_in, wide_in,
            wide_in, head_in, head_in, wide_in, V((16, 4 * H * D), BF),
            V((2, R, H * D), F32),
            V((4, R, D), F32),
            V((2 * HALF, 2 * D), BF),
            V((2 * ROWS, D), BF),
            V((2 * ROWS, D), BF),
            V((R, H * D), BF),
            V((2 * HALF, 2 * ROWS), F32),
            V((R, ROWS), F32),
            V((2 * HALF - EARLY * 512, 2 * ROWS), BF),
            V((8, 2 * ROWS), F32),
            V((8, 2 * ROWS), F32),
            V((D, 2 * ROWS), F32),
            V((512, 2 * D), F32),
            V((BLK, 2 * D), F32),
            V((BLK, 2 * D), F32),
            V((4, BLK, 2 * D), BF),
            V((3, BLK, 2 * D), BF),
            V((4, BLK, 2 * D), BF),
            V((3, BLK, 2 * D), BF),
            V((NU, BLK, 2 * D), BF),
            V((NU, BLK, 2 * D), BF),
            V((BLK, 2 * D), BF),
            V((NU, S, 2 * D), BF),
            V((BLK, 2 * D), BF),
            V((NZ, S, 2 * D), BF),
            pltpu.SemaphoreType.DMA((COPIES,)),
            pltpu.SemaphoreType.DMA((COPIES,)),
            pltpu.SemaphoreType.DMA((10,)),
            pltpu.SemaphoreType.DMA((3,)),
        ],
        compiler_params=pltpu.CompilerParams(
            collective_id=0, has_side_effects=True, vmem_limit_bytes=63 * 2**20
        ),
    )(
        prompt_q, prompt_k, prompt_v, prompt_out, prompt_dout,
        resp_q, resp_k, resp_v, resp_out, resp_dout, resp_len, loss_mask.reshape(1, R),
    )
    return pl.pallas_call(
        hand_out,
        out_shape=[wide_out, head_out, head_out, wide_out, head_out, head_out],
        in_specs=[vmem] * 2,
        out_specs=[vmem] * 6,
    )(*sums)


def solution(mesh):
    grid = P("wide", "kv")
    return jax.shard_map(
        local,
        mesh=mesh,
        in_specs=(grid,) * 9 + (P(("wide", "kv"), None), P("wide"), P("wide")),
        out_specs=(grid,) * 6,
        check_vma=False,
    )
```

```python
import functools
import math

import jax
import jax.numpy as jnp
from jax import lax
from jax.experimental import pallas as pl
from jax.experimental.pallas import tpu as pltpu
from jax.sharding import PartitionSpec as P

MESH = pl.DeviceIdType.MESH
BF = jnp.bfloat16
F32 = jnp.float32
NX, NZ, NY = 4, 8, 2
NU = NX * NY
R = 64
S = R // 2
D = 128
H = 16
ROWS = H * R
SCALE = 1.0 / math.sqrt(D)
EXP2_SCALE = math.log2(math.e) / math.sqrt(D)
HALF = NU * NZ * S
BLK = NU * S
SUBS = NX
PIECE = BLK // SUBS
SUMS = 2
SUM_PIECE = BLK // SUMS
NN = (((1,), (0,)), ((), ()))
NT = (((1,), (1,)), ((), ()))
TN = (((0,), (0,)), ((), ()))
COPIES = 87


def dot(a, b, dims):
    return lax.dot_general(a, b, dims, preferred_element_type=F32)


def by_head(ref):
    return jnp.concatenate([ref[:, h * D : (h + 1) * D] for h in range(H)], axis=0)


def lane_dots(a, b):
    prod = a.astype(F32) * b.astype(F32)
    high = prod.astype(BF)
    low = (prod - high.astype(F32)).astype(BF)
    ones = jnp.ones((8, D), BF)
    return dot(ones, high, NT) + dot(ones, low, NT)


def kernel(
    pq_hbm, pk_hbm, pv_hbm, po_hbm, pdo_hbm, rq_hbm, rk_hbm, rv_hbm, ro_hbm, rdo_hbm, rlen, lmask,
    dq_hbm, kvg_hbm,
    pk, pv, rk, rv, rdo, dq, kvg,
    kvb, qs, dos, e, eo, dss, zs, dvec, dqt, part, acc_p, acc_q,
    s_r, s_l, r_r, r_l, sq, rq_in, sp_out, rp_in, sz_out, rz_in,
    ssem, rsem, lsem, osem,
):
    w, kv = lax.axis_index("wide"), lax.axis_index("kv")
    x, z, y = w // (NZ * NY), lax.rem(w // NY, NZ), lax.rem(w, NY)
    u = x * NY + y

    def dev(uu, zz, vv):
        return (((uu // NY) * NZ + zz) * NY + lax.rem(uu, NY), vv)

    def u_to(i):
        return lax.rem(x + i // NY, NX) * NY + lax.rem(y + lax.rem(i, NY), NY)

    def u_from(i):
        return lax.rem(x + NX - i // NY, NX) * NY + lax.rem(y + lax.rem(i, NY), NY)

    def up(i):
        return dev(u_to(i), z, kv)

    def zp(i):
        return dev(u, lax.rem(z + i, NZ), kv)

    def vp(i):
        return dev(u, z, lax.rem(kv + i, 4))

    barrier = pltpu.get_barrier_semaphore()
    peers = [zp(i) for i in range(1, NZ)] + [up(i) for i in range(1, NU)] + [vp(i) for i in range(1, 4)]
    for peer in peers:
        pl.semaphore_signal(barrier, inc=1, device_id=peer, device_id_type=MESH)

    pq, po, pdo, rq, ro, arrived = (dss.at[pl.ds(i * R, R)] for i in range(6))
    hbm = (pk_hbm, pv_hbm, rq_hbm, rk_hbm, pq_hbm, pdo_hbm, po_hbm, rdo_hbm, ro_hbm, rv_hbm)
    loads = [
        pltpu.make_async_copy(src, dst, lsem.at[i])
        for i, (src, dst) in enumerate(zip(hbm, (pk, pv, rq, rk, pq, pdo, po, rdo, ro, rv), strict=True))
    ]
    for load in loads:
        load.start()

    sem_no = {}

    def copy(key, src, dst, to):
        i = sem_no.setdefault(key, len(sem_no))
        return pltpu.make_async_remote_copy(
            src_ref=src, dst_ref=dst, send_sem=ssem.at[i], recv_sem=rsem.at[i],
            device_id=to, device_id_type=MESH,
        )

    def rows(off, n):
        return kvb.at[pl.ds(pl.multiple_of(off, S), n)]

    own_p = z * BLK + u * S
    own_q = HALF + u * BLK + z * S

    def g_pu(i):
        return copy(("gpu", i), rows(own_p, S), rows(own_p, S), up(i))

    def g_qz(i):
        return copy(("gqz", i), rows(own_q, S), rows(own_q, S), zp(i))

    def g_pz(right, s, k):
        at = lax.rem(x + NX - k, NX)
        b = rows(lax.rem(z + (NZ - s if right else s), NZ) * BLK + at * PIECE, PIECE)
        return copy(("gpz", right, s, k), b, b, zp(1 if right else NZ - 1))

    def g_qu(i):
        return copy(("gqu", i), rows(HALF + u * BLK, BLK), rows(HALF + u * BLK, BLK), up(i))

    def g_v(i):
        col = pl.multiple_of(lax.rem(kv + i, 4) * (H * D), H * D)
        return copy(
            ("gv", i),
            rdo.at[:, pl.ds(col, H * D)],
            arrived.at[pl.ds(pl.multiple_of(kv * 16, 16), 16)],
            vp(i),
        )

    def pieces(right, s):
        if s < NZ // 2 - 1:
            return range(SUBS)
        return range(SUBS // 2) if right else range(SUBS // 2, SUBS)

    def t_pz(right, t, k):
        part_of = pl.ds(k * SUM_PIECE, SUM_PIECE)
        if right:
            return copy(("tpr", t, k), s_r.at[t, part_of], r_r.at[t, part_of], zp(1))
        return copy(("tpl", t, k), s_l.at[t, part_of], r_l.at[t, part_of], zp(NZ - 1))

    def t_qu(i):
        return copy(("tqu", i), sq.at[i], rq_in.at[i], up(i))

    def t_pu(i):
        src = sp_out.at[pl.ds(pl.multiple_of(u_to(i) * S, S), S)]
        return copy(("tpu", i), src, rp_in.at[i], up(i))

    def t_qz(i):
        src = sz_out.at[pl.ds(pl.multiple_of(lax.rem(z + i, NZ) * S, S), S)]
        return copy(("tqz", i), src, rz_in.at[i], zp(i))

    for load in loads:
        load.wait()
    for off, first_row in ((own_p, 0), (own_q, S)):
        kvb[pl.ds(pl.multiple_of(off, S), S), 0:D] = pk[first_row : first_row + S, :]
        kvb[pl.ds(pl.multiple_of(off, S), S), D : 2 * D] = pv[first_row : first_row + S, :]
    qs[0:ROWS] = by_head(pq)
    qs[ROWS : 2 * ROWS] = by_head(rq)
    prompt_cot = by_head(pdo)
    dos[0:ROWS] = prompt_cot
    dvec[:, 0:ROWS] = lane_dots(prompt_cot, by_head(po))
    dqt[...] = jnp.zeros_like(dqt)
    row_minus_col = lax.broadcasted_iota(jnp.int32, (R, ROWS), 0) - lax.rem(
        lax.broadcasted_iota(jnp.int32, (R, ROWS), 1), R
    )
    own_e = jnp.where(
        row_minus_col <= 0, jnp.exp2(dot(rk[...], qs[ROWS : 2 * ROWS], NT) * EXP2_SCALE), 0.0
    )
    eo[...] = own_e
    zs[:, 0:ROWS] = jnp.zeros((8, ROWS), F32)
    zs[:, ROWS : 2 * ROWS] = jnp.sum(own_e.reshape(R // 8, 8, ROWS), axis=0)
    pl.semaphore_wait(barrier, len(peers))

    for i in range(1, NU):
        g_pu(i).start()
    for i in (4, 3, 5, 2, 6, 1, 7):
        g_qz(i).start()
    for i in range(1, 4):
        g_v(i).start()
    arrived[pl.ds(pl.multiple_of(kv * 16, 16), 16), :] = rdo[:, pl.ds(pl.multiple_of(kv * (H * D), H * D), H * D)]
    for k in range(SUBS):
        for i in range(NY * k, NY * (k + 1)):
            if i > 0:
                g_pu(i).wait_recv()
        g_pz(True, 0, k).start()
        g_pz(False, 0, k).start()
    for i in range(1, NZ):
        g_qz(i).wait_recv()
    for i in range(1, NU):
        g_qu(i).start()

    def response_cotangents():
        for i in range(1, 4):
            g_v(i).wait_recv()
        tokens = lax.broadcasted_iota(jnp.int32, (R, R), 1)
        usable = (lmask[...] == 1) & (lax.broadcasted_iota(jnp.int32, (1, R), 1) < rlen[...])
        diagonal = lax.broadcasted_iota(jnp.int32, (R, R), 0) == tokens
        keep = jnp.sum(jnp.where(diagonal & usable, 1.0, 0.0), axis=1, keepdims=True)
        keep = jnp.broadcast_to(keep, (R, D)) > 0.5
        keep = jnp.concatenate([keep] * H, axis=0)
        cot = jnp.where(keep, by_head(arrived).astype(F32), 0.0).astype(BF)
        dos[ROWS : 2 * ROWS] = cot
        dvec[:, ROWS : 2 * ROWS] = lane_dots(cot, by_head(ro))

    def first(j, carry):
        for s in range(NZ // 2):

            @pl.when(j == (s + 1 if s < NZ // 2 - 1 else 7))
            def _():
                for k in range(SUBS):
                    for right in (True, False):
                        if k in pieces(right, s):
                            g_pz(right, s, k).wait_recv()
                            if s < NZ // 2 - 1 and k in pieces(right, s + 1):
                                g_pz(right, s + 1, k).start()
                if s == NZ // 2 - 1:
                    g_qu(NU - 1).wait_recv()

        @pl.when(j == NU // 2)
        def _():
            response_cotangents()

        for c in range(1, NU // 2):

            @pl.when(j == NU // 2 - 1 + c)
            def _():
                g_qu(2 * c - 1).wait_recv()
                g_qu(2 * c).wait_recv()

        q, opening, closing = j // 4, 1 - (j + 7) // 8, j // 7
        p1, p2 = 1 - q + closing, (1 - q) * (1 - opening)
        z1 = lax.rem(z + NZ - j * (1 - q) - 4 * closing, NZ)
        z2 = lax.rem(z + j, NZ)
        u1 = u_from(lax.rem(2 * NU + 2 * j - 7, NU))
        u2 = u_from(q * (2 * j - 6) - closing)
        off1 = p1 * (z1 * BLK) + (1 - p1) * (HALF + u1 * BLK)
        off2 = p2 * (z2 * BLK) + (1 - p2) * (HALF + u2 * BLK)
        off1, off2 = pl.multiple_of(off1, BLK), pl.multiple_of(off2, BLK)
        keys = jnp.concatenate([kvb[pl.ds(off1, 256), 0:D], kvb[pl.ds(off2, 256), 0:D]], axis=0)
        ex = jnp.exp2(dot(keys, qs[...], NT) * EXP2_SCALE)
        seen = []
        for p, zz, uu, top in ((p1, z1, u1, 0), (p2, z2, u2, BLK)):
            for g in range(8):
                in_p = (g // NY) * (NZ * NY) + zz * NY + g % NY
                in_q = (uu // NY) * (NZ * NY) + g * NY + lax.rem(uu, NY)
                limit = (w - (p * in_p + (1 - p) * in_q)) * R - (1 - p) * S
                block = ex[top + g * S : top + (g + 1) * S, 0:ROWS]
                seen.append(jnp.where(row_minus_col[0:S] <= limit, block, 0.0))
        seen = jnp.concatenate(seen, axis=0)
        rest = ex[:, ROWS : 2 * ROWS]
        for k, off in ((0, off1), (1, off2)):
            e[pl.ds(off, 256), 0:ROWS] = seen[k * 256 : (k + 1) * 256]
            e[pl.ds(off, 256), ROWS : 2 * ROWS] = rest[k * 256 : (k + 1) * 256]
        zs[:, 0:ROWS] += jnp.sum(seen.reshape(64, 8, ROWS), axis=0)
        zs[:, ROWS : 2 * ROWS] += jnp.sum(rest.reshape(64, 8, ROWS), axis=0)
        return carry

    lax.fori_loop(0, 8, first, 0)

    zs[...] = jnp.broadcast_to(1.0 / jnp.sum(zs[...], axis=0, keepdims=True), zs.shape)

    def chunk(j):
        t, mixed, odd = j // 2, j // 6, lax.rem(j, 2)
        p1, p2 = (1 - mixed) * (1 - odd) + mixed, (1 - mixed) * (1 - odd)
        z1, z2 = lax.rem(z + 4 - t - mixed * odd, NZ), lax.rem(z + 5 + t, NZ)
        u1, u2 = u_to(2 * t + 1), u_to(lax.rem(2 * t + 2 - mixed * (1 - odd), NU))
        off1 = p1 * (z1 * BLK) + (1 - p1) * (HALF + u1 * BLK)
        off2 = p2 * (z2 * BLK) + (1 - p2) * (HALF + u2 * BLK)
        return pl.multiple_of(off1, BLK), pl.multiple_of(off2, BLK)

    def second(j, carry):
        off1, off2 = chunk(j)
        for off, top in ((off1, 0), (off2, BLK)):
            weights = e[pl.ds(off, BLK), :] * zs[0:1, :]
            part[top : top + BLK, D : 2 * D] = dot(weights.astype(BF), dos[...], NN)
            weight_grad = dot(kvb[pl.ds(off, BLK), D : 2 * D], dos[...], NT)
            score_grad = (weights * (weight_grad - dvec[0:1, :])).astype(BF)
            dss[pl.ds(pl.multiple_of(j * (2 * BLK), 2 * BLK) + top, BLK), :] = score_grad
            part[top : top + BLK, 0:D] = dot(score_grad, qs[...], NN)

        for t in range(3):

            @pl.when(j == 2 * t)
            def _():
                for k in range(SUMS):
                    piece = pl.ds(k * SUM_PIECE, SUM_PIECE)
                    right = part[k * SUM_PIECE : (k + 1) * SUM_PIECE, :]
                    left = part[BLK + k * SUM_PIECE : BLK + (k + 1) * SUM_PIECE, :]
                    if t > 0:
                        t_pz(True, t - 1, k).wait_recv()
                        right = right + r_r[t - 1, piece].astype(F32)
                    s_r[t, piece] = right.astype(BF)
                    t_pz(True, t, k).start()
                    if t > 0:
                        t_pz(False, t - 1, k).wait_recv()
                        left = left + r_l[t - 1, piece].astype(F32)
                    s_l[t, piece] = left.astype(BF)
                    t_pz(False, t, k).start()

            @pl.when(j == 2 * t + 1)
            def _():
                sq[2 * t + 1] = part[0:BLK, :].astype(BF)
                t_qu(2 * t + 1).start()
                sq[2 * t + 2] = part[BLK : 2 * BLK, :].astype(BF)
                t_qu(2 * t + 2).start()

        @pl.when(j == 6)
        def _():
            sq[NU - 1] = part[BLK : 2 * BLK, :].astype(BF)
            t_qu(NU - 1).start()
            for k in range(SUMS):
                piece = pl.ds(k * SUM_PIECE, SUM_PIECE)
                t_pz(True, 2, k).wait_recv()
                s_r[3, piece] = (part[k * SUM_PIECE : (k + 1) * SUM_PIECE, :] + r_r[2, piece].astype(F32)).astype(BF)
                t_pz(True, 3, k).start()

        @pl.when(j == 7)
        def _():
            acc_p[...] = part[0:BLK, :]
            acc_q[...] = part[BLK : 2 * BLK, :]

        return carry

    lax.fori_loop(0, 8, second, 0)

    def late(i, carry):
        off1, off2 = chunk(i)
        keys = jnp.concatenate([kvb[pl.ds(off1, 256), 0:D], kvb[pl.ds(off2, 256), 0:D]], axis=0)
        dqt[...] += dot(keys, dss[pl.ds(pl.multiple_of(i * 512, 512), 512), :], TN)

        @pl.when(i == 1)
        def _():
            total = acc_q[...]
            for k in range(1, NU):
                t_qu(k).wait_recv()
                total = total + rq_in[k].astype(F32)
            acc_q[...] = total
            sz_out[...] = total.astype(BF)
            for k in (4, 3, 5, 2, 6, 1, 7):
                t_qz(k).start()

        @pl.when(i == 2)
        def _():
            total = acc_p[...]
            for k in range(SUMS):
                t_pz(True, 3, k).wait_recv()
                t_pz(False, 2, k).wait_recv()
            total = total + r_r[3].astype(F32) + r_l[2].astype(F32)
            acc_p[...] = total
            sp_out[...] = total.astype(BF)
            for k in range(1, NU):
                t_pu(k).start()

        return carry

    lax.fori_loop(0, 8, late, 0)

    own_w = eo[...] * zs[0:1, ROWS : 2 * ROWS]
    kvg[3] = dot(own_w.astype(BF), dos[ROWS : 2 * ROWS], NN)
    own_g = dot(rv[...], dos[ROWS : 2 * ROWS], NT) - dvec[0:1, ROWS : 2 * ROWS]
    own_g = (own_w * own_g).astype(BF)
    kvg[2] = dot(own_g, qs[ROWS : 2 * ROWS], NN) * SCALE
    dqt[:, ROWS : 2 * ROWS] += dot(rk[...], own_g, TN)

    stores = [
        pltpu.make_async_copy(dq.at[0], dq_hbm.at[0], osem.at[0]),
        pltpu.make_async_copy(dq.at[1], dq_hbm.at[1], osem.at[1]),
        pltpu.make_async_copy(kvg, kvg_hbm, osem.at[2]),
    ]
    for which, first_col in ((0, 0), (1, ROWS)):
        for h in range(0, H, 2):
            block = dqt[:, first_col + h * R : first_col + (h + 2) * R].T * SCALE
            dq[which, :, h * D : (h + 1) * D] = block[0:R]
            dq[which, :, (h + 1) * D : (h + 2) * D] = block[R : 2 * R]
        stores[which].start()

    for i in range(1, NU):
        t_qz(i).wait_recv()
        t_pu(i).wait_recv()
    for acc, arrivals, place, first_row in ((acc_p, rp_in, u, 0), (acc_q, rz_in, z, S)):
        total = acc[pl.ds(pl.multiple_of(place * S, S), S), :]
        for i in range(1, NU):
            total = total + arrivals[i].astype(F32)
        kvg[0, first_row : first_row + S, :] = total[:, 0:D] * SCALE
        kvg[1, first_row : first_row + S, :] = total[:, D : 2 * D]
    stores[2].start()

    for i in range(1, NU):
        for sent in (g_pu, g_qz, g_qu, t_qu, t_pu, t_qz):
            sent(i).wait_send()
    for i in range(1, 4):
        g_v(i).wait_send()
    for right in (True, False):
        for s in range(NZ // 2):
            for k in pieces(right, s):
                g_pz(right, s, k).wait_send()
            if right or s < 3:
                for k in range(SUMS):
                    t_pz(right, s, k).wait_send()
    for store in stores:
        store.wait()


def hand_out(dq, kvg, pdq, pdk, pdv, rdq, rdk, rdv):
    pdq[...] = dq[0]
    rdq[...] = dq[1]
    for i, out in enumerate((pdk, pdv, rdk, rdv)):
        out[...] = kvg[i]


def local(
    prompt_q, prompt_k, prompt_v, prompt_out, prompt_dout,
    resp_q, resp_k, resp_v, resp_out, resp_dout, resp_len, loss_mask,
):
    vmem = pl.BlockSpec(memory_space=pltpu.VMEM)
    anywhere = pl.BlockSpec(memory_space=pl.ANY)
    wide_out = jax.ShapeDtypeStruct((R, H * D), F32)
    head_out = jax.ShapeDtypeStruct((R, D), F32)
    V = pltpu.VMEM
    head_in = V((R, D), BF)
    sums = pl.pallas_call(
        kernel,
        out_shape=[jax.ShapeDtypeStruct((2, R, H * D), F32), jax.ShapeDtypeStruct((4, R, D), F32)],
        in_specs=[anywhere] * 10 + [vmem] * 2,
        out_specs=[anywhere] * 2,
        scratch_shapes=[
            head_in, head_in, head_in, head_in, V((16, 4 * H * D), BF),
            V((2, R, H * D), F32),
            V((4, R, D), F32),
            V((2 * HALF, 2 * D), BF),
            V((2 * ROWS, D), BF),
            V((2 * ROWS, D), BF),
            V((2 * HALF, 2 * ROWS), F32),
            V((R, ROWS), F32),
            V((2 * HALF, 2 * ROWS), BF),
            V((8, 2 * ROWS), F32),
            V((8, 2 * ROWS), F32),
            V((D, 2 * ROWS), F32),
            V((512, 2 * D), F32),
            V((BLK, 2 * D), F32),
            V((BLK, 2 * D), F32),
            V((4, BLK, 2 * D), BF),
            V((3, BLK, 2 * D), BF),
            V((4, BLK, 2 * D), BF),
            V((3, BLK, 2 * D), BF),
            V((NU, BLK, 2 * D), BF),
            V((NU, BLK, 2 * D), BF),
            V((BLK, 2 * D), BF),
            V((NU, S, 2 * D), BF),
            V((BLK, 2 * D), BF),
            V((NZ, S, 2 * D), BF),
            pltpu.SemaphoreType.DMA((COPIES,)),
            pltpu.SemaphoreType.DMA((COPIES,)),
            pltpu.SemaphoreType.DMA((10,)),
            pltpu.SemaphoreType.DMA((3,)),
        ],
        compiler_params=pltpu.CompilerParams(
            collective_id=0, has_side_effects=True, vmem_limit_bytes=127 * 2**19
        ),
    )(
        prompt_q, prompt_k, prompt_v, prompt_out, prompt_dout,
        resp_q, resp_k, resp_v, resp_out, resp_dout, resp_len.reshape(1, 1), loss_mask.reshape(1, R),
    )
    return pl.pallas_call(
        hand_out,
        out_shape=[wide_out, head_out, head_out, wide_out, head_out, head_out],
        in_specs=[vmem] * 2,
        out_specs=[vmem] * 6,
    )(*sums)


def solution(mesh):
    grid = P("wide", "kv")
    return jax.shard_map(
        local,
        mesh=mesh,
        in_specs=(grid,) * 9 + (P(("wide", "kv"), None), P("wide"), P("wide")),
        out_specs=(grid,) * 6,
        check_vma=False,
    )
```

```python
import functools
import math

import jax
import jax.numpy as jnp
from jax import lax
from jax.experimental import pallas as pl
from jax.experimental.pallas import tpu as pltpu
from jax.sharding import PartitionSpec as P

MESH = pl.DeviceIdType.MESH
BF = jnp.bfloat16
F32 = jnp.float32
NX, NZ, NY = 4, 8, 2
NU = NX * NY
R = 64
S = R // 2
D = 128
H = 16
ROWS = H * R
SCALE = 1.0 / math.sqrt(D)
EXP2_SCALE = math.log2(math.e) / math.sqrt(D)
HALF = NU * NZ * S
BLK = NU * S
SUBS = NX
PIECE = BLK // SUBS
SUMS = 2
SUM_PIECE = BLK // SUMS
NN = (((1,), (0,)), ((), ()))
NT = (((1,), (1,)), ((), ()))
TN = (((0,), (0,)), ((), ()))
COPIES = 87


def dot(a, b, dims):
    return lax.dot_general(a, b, dims, preferred_element_type=F32)


def by_head(ref):
    return jnp.concatenate([ref[:, h * D : (h + 1) * D] for h in range(H)], axis=0)


def lane_dots(a, b):
    prod = a.astype(F32) * b.astype(F32)
    high = prod.astype(BF)
    low = (prod - high.astype(F32)).astype(BF)
    ones = jnp.ones((8, D), BF)
    return dot(ones, high, NT) + dot(ones, low, NT)


def kernel(
    pq_hbm, pk_hbm, pv_hbm, po_hbm, pdo_hbm, rq_hbm, rk_hbm, rv_hbm, ro_hbm, rdo_hbm, rlen, lmask,
    dq_hbm, kvg_hbm,
    pk, pv, rk, rv, rdo, dq, kvg,
    kvb, qs, dos, e, eo, dss, zs, dvec, dqt, part, acc_p, acc_q,
    s_r, s_l, r_r, r_l, sq, rq_in, sp_out, rp_in, sz_out, rz_in,
    ssem, rsem, lsem, osem,
):
    w, kv = lax.axis_index("wide"), lax.axis_index("kv")
    x, z, y = w // (NZ * NY), lax.rem(w // NY, NZ), lax.rem(w, NY)
    u = x * NY + y

    def dev(uu, zz, vv):
        return (((uu // NY) * NZ + zz) * NY + lax.rem(uu, NY), vv)

    def u_to(i):
        return lax.rem(x + i // NY, NX) * NY + lax.rem(y + lax.rem(i, NY), NY)

    def u_from(i):
        return lax.rem(x + NX - i // NY, NX) * NY + lax.rem(y + lax.rem(i, NY), NY)

    def up(i):
        return dev(u_to(i), z, kv)

    def zp(i):
        return dev(u, lax.rem(z + i, NZ), kv)

    def vp(i):
        return dev(u, z, lax.rem(kv + i, 4))

    barrier = pltpu.get_barrier_semaphore()
    peers = [zp(i) for i in range(1, NZ)] + [up(i) for i in range(1, NU)] + [vp(i) for i in range(1, 4)]
    for peer in peers:
        pl.semaphore_signal(barrier, inc=1, device_id=peer, device_id_type=MESH)

    pq, po, pdo, rq, ro, arrived = (dss.at[pl.ds(i * R, R)] for i in range(6))
    hbm = (pk_hbm, pv_hbm, rq_hbm, rk_hbm, pq_hbm, pdo_hbm, po_hbm, rdo_hbm, ro_hbm, rv_hbm)
    loads = [
        pltpu.make_async_copy(src, dst, lsem.at[i])
        for i, (src, dst) in enumerate(zip(hbm, (pk, pv, rq, rk, pq, pdo, po, rdo, ro, rv), strict=True))
    ]
    for load in loads:
        load.start()

    sem_no = {}

    def copy(key, src, dst, to):
        i = sem_no.setdefault(key, len(sem_no))
        return pltpu.make_async_remote_copy(
            src_ref=src, dst_ref=dst, send_sem=ssem.at[i], recv_sem=rsem.at[i],
            device_id=to, device_id_type=MESH,
        )

    def rows(off, n):
        return kvb.at[pl.ds(pl.multiple_of(off, S), n)]

    own_p = z * BLK + u * S
    own_q = HALF + u * BLK + z * S

    def g_pu(i):
        return copy(("gpu", i), rows(own_p, S), rows(own_p, S), up(i))

    def g_qz(i):
        return copy(("gqz", i), rows(own_q, S), rows(own_q, S), zp(i))

    def g_pz(right, s, k):
        at = lax.rem(x + NX - k, NX)
        b = rows(lax.rem(z + (NZ - s if right else s), NZ) * BLK + at * PIECE, PIECE)
        return copy(("gpz", right, s, k), b, b, zp(1 if right else NZ - 1))

    def g_qu(i):
        return copy(("gqu", i), rows(HALF + u * BLK, BLK), rows(HALF + u * BLK, BLK), up(i))

    def g_v(i):
        col = pl.multiple_of(lax.rem(kv + i, 4) * (H * D), H * D)
        return copy(
            ("gv", i),
            rdo.at[:, pl.ds(col, H * D)],
            arrived.at[pl.ds(pl.multiple_of(kv * 16, 16), 16)],
            vp(i),
        )

    def pieces(right, s):
        if s < NZ // 2 - 1:
            return range(SUBS)
        return range(SUBS // 2) if right else range(SUBS // 2, SUBS)

    def t_pz(right, t, k):
        part_of = pl.ds(k * SUM_PIECE, SUM_PIECE)
        if right:
            return copy(("tpr", t, k), s_r.at[t, part_of], r_r.at[t, part_of], zp(1))
        return copy(("tpl", t, k), s_l.at[t, part_of], r_l.at[t, part_of], zp(NZ - 1))

    def t_qu(i):
        return copy(("tqu", i), sq.at[i], rq_in.at[i], up(i))

    def t_pu(i):
        src = sp_out.at[pl.ds(pl.multiple_of(u_to(i) * S, S), S)]
        return copy(("tpu", i), src, rp_in.at[i], up(i))

    def t_qz(i):
        src = sz_out.at[pl.ds(pl.multiple_of(lax.rem(z + i, NZ) * S, S), S)]
        return copy(("tqz", i), src, rz_in.at[i], zp(i))

    for load in loads:
        load.wait()
    for off, first_row in ((own_p, 0), (own_q, S)):
        kvb[pl.ds(pl.multiple_of(off, S), S), 0:D] = pk[first_row : first_row + S, :]
        kvb[pl.ds(pl.multiple_of(off, S), S), D : 2 * D] = pv[first_row : first_row + S, :]
    qs[0:ROWS] = by_head(pq)
    qs[ROWS : 2 * ROWS] = by_head(rq)
    prompt_cot = by_head(pdo)
    dos[0:ROWS] = prompt_cot
    dvec[:, 0:ROWS] = lane_dots(prompt_cot, by_head(po))
    dqt[...] = jnp.zeros_like(dqt)
    row_minus_col = lax.broadcasted_iota(jnp.int32, (R, ROWS), 0) - lax.rem(
        lax.broadcasted_iota(jnp.int32, (R, ROWS), 1), R
    )
    own_e = jnp.where(
        row_minus_col <= 0, jnp.exp2(dot(rk[...], qs[ROWS : 2 * ROWS], NT) * EXP2_SCALE), 0.0
    )
    eo[...] = own_e
    zs[:, 0:ROWS] = jnp.zeros((8, ROWS), F32)
    zs[:, ROWS : 2 * ROWS] = jnp.sum(own_e.reshape(R // 8, 8, ROWS), axis=0)
    pl.semaphore_wait(barrier, len(peers))

    for i in range(1, NU):
        g_pu(i).start()
    for i in (4, 3, 5, 2, 6, 1, 7):
        g_qz(i).start()
    for i in range(1, 4):
        g_v(i).start()
    arrived[pl.ds(pl.multiple_of(kv * 16, 16), 16), :] = rdo[:, pl.ds(pl.multiple_of(kv * (H * D), H * D), H * D)]
    for k in range(SUBS):
        for i in range(NY * k, NY * (k + 1)):
            if i > 0:
                g_pu(i).wait_recv()
        g_pz(True, 0, k).start()
        g_pz(False, 0, k).start()
    for i in range(1, NZ):
        g_qz(i).wait_recv()
    for i in range(1, NU):
        g_qu(i).start()

    def response_cotangents():
        for i in range(1, 4):
            g_v(i).wait_recv()
        tokens = lax.broadcasted_iota(jnp.int32, (R, R), 1)
        usable = (lmask[...] == 1) & (lax.broadcasted_iota(jnp.int32, (1, R), 1) < rlen[...])
        diagonal = lax.broadcasted_iota(jnp.int32, (R, R), 0) == tokens
        keep = jnp.sum(jnp.where(diagonal & usable, 1.0, 0.0), axis=1, keepdims=True)
        keep = jnp.broadcast_to(keep, (R, D)) > 0.5
        keep = jnp.concatenate([keep] * H, axis=0)
        cot = jnp.where(keep, by_head(arrived).astype(F32), 0.0).astype(BF)
        dos[ROWS : 2 * ROWS] = cot
        dvec[:, ROWS : 2 * ROWS] = lane_dots(cot, by_head(ro))

    def first(j, carry):
        for s in range(NZ // 2):

            @pl.when(j == (s + 1 if s < NZ // 2 - 1 else 7))
            def _():
                for k in range(SUBS):
                    for right in (True, False):
                        if k in pieces(right, s):
                            g_pz(right, s, k).wait_recv()
                            if s < NZ // 2 - 1 and k in pieces(right, s + 1):
                                g_pz(right, s + 1, k).start()
                if s == NZ // 2 - 1:
                    g_qu(NU - 1).wait_recv()

        @pl.when(j == NU // 2)
        def _():
            response_cotangents()

        for c in range(1, NU // 2):

            @pl.when(j == NU // 2 - 1 + c)
            def _():
                g_qu(2 * c - 1).wait_recv()
                g_qu(2 * c).wait_recv()

        q, opening, closing = j // 4, 1 - (j + 7) // 8, j // 7
        p1, p2 = 1 - q + closing, (1 - q) * (1 - opening)
        z1 = lax.rem(z + NZ - j * (1 - q) - 4 * closing, NZ)
        z2 = lax.rem(z + j, NZ)
        u1 = u_from(lax.rem(2 * NU + 2 * j - 7, NU))
        u2 = u_from(q * (2 * j - 6) - closing)
        off1 = p1 * (z1 * BLK) + (1 - p1) * (HALF + u1 * BLK)
        off2 = p2 * (z2 * BLK) + (1 - p2) * (HALF + u2 * BLK)
        off1, off2 = pl.multiple_of(off1, BLK), pl.multiple_of(off2, BLK)
        keys = jnp.concatenate([kvb[pl.ds(off1, 256), 0:D], kvb[pl.ds(off2, 256), 0:D]], axis=0)
        ex = jnp.exp2(dot(keys, qs[...], NT) * EXP2_SCALE)
        seen = []
        for p, zz, uu, top in ((p1, z1, u1, 0), (p2, z2, u2, BLK)):
            for g in range(8):
                in_p = (g // NY) * (NZ * NY) + zz * NY + g % NY
                in_q = (uu // NY) * (NZ * NY) + g * NY + lax.rem(uu, NY)
                limit = (w - (p * in_p + (1 - p) * in_q)) * R - (1 - p) * S
                block = ex[top + g * S : top + (g + 1) * S, 0:ROWS]
                seen.append(jnp.where(row_minus_col[0:S] <= limit, block, 0.0))
        seen = jnp.concatenate(seen, axis=0)
        rest = ex[:, ROWS : 2 * ROWS]
        for k, off in ((0, off1), (1, off2)):
            e[pl.ds(off, 256), 0:ROWS] = seen[k * 256 : (k + 1) * 256]
            e[pl.ds(off, 256), ROWS : 2 * ROWS] = rest[k * 256 : (k + 1) * 256]
        zs[:, 0:ROWS] += jnp.sum(seen.reshape(64, 8, ROWS), axis=0)
        zs[:, ROWS : 2 * ROWS] += jnp.sum(rest.reshape(64, 8, ROWS), axis=0)
        return carry

    lax.fori_loop(0, 8, first, 0)

    zs[...] = jnp.broadcast_to(1.0 / jnp.sum(zs[...], axis=0, keepdims=True), zs.shape)

    def chunk(j):
        odd, from_5, from_6, last = lax.rem(j, 2), j // 5, j // 6, j // 7
        p1 = 1 - odd + last
        p2 = (1 - odd) * (1 - (j // 4) * (1 - from_5))
        z1, z2 = lax.rem(z + 4 - j // 2 - last, NZ), lax.rem(z + 5 + j // 2 - from_6, NZ)
        u1, u2 = u_to(8 - j - from_5), u_to(7 - j - from_5 + last)
        off1 = p1 * (z1 * BLK) + (1 - p1) * (HALF + u1 * BLK)
        off2 = p2 * (z2 * BLK) + (1 - p2) * (HALF + u2 * BLK)
        return pl.multiple_of(off1, BLK), pl.multiple_of(off2, BLK)

    def second(j, carry):
        off1, off2 = chunk(j)
        for off, top in ((off1, 0), (off2, BLK)):
            weights = e[pl.ds(off, BLK), :] * zs[0:1, :]
            part[top : top + BLK, D : 2 * D] = dot(weights.astype(BF), dos[...], NN)
            weight_grad = dot(kvb[pl.ds(off, BLK), D : 2 * D], dos[...], NT)
            score_grad = (weights * (weight_grad - dvec[0:1, :])).astype(BF)
            dss[pl.ds(pl.multiple_of(j * (2 * BLK), 2 * BLK) + top, BLK), :] = score_grad
            part[top : top + BLK, 0:D] = dot(score_grad, qs[...], NN)

        def send_p(right, t, top):
            sent, arrived_sum = (s_r, r_r) if right else (s_l, r_l)
            for k in range(SUMS):
                piece = pl.ds(k * SUM_PIECE, SUM_PIECE)
                value = part[top + k * SUM_PIECE : top + (k + 1) * SUM_PIECE, :]
                if t > 0:
                    t_pz(right, t - 1, k).wait_recv()
                    value = value + arrived_sum[t - 1, piece].astype(F32)
                sent[t, piece] = value.astype(BF)
                t_pz(right, t, k).start()

        def send_q(i, top):
            sq[i] = part[top : top + BLK, :].astype(BF)
            t_qu(i).start()

        @pl.when(j == 0)
        def _():
            send_p(True, 0, 0)
            send_p(False, 0, BLK)

        @pl.when(j == 1)
        def _():
            send_q(7, 0)
            send_q(6, BLK)

        @pl.when(j == 2)
        def _():
            send_p(True, 1, 0)
            send_p(False, 1, BLK)

        @pl.when(j == 3)
        def _():
            send_q(5, 0)
            send_q(4, BLK)

        @pl.when(j == 4)
        def _():
            send_q(3, BLK)
            send_p(True, 2, 0)

        @pl.when(j == 5)
        def _():
            send_q(2, 0)
            send_q(1, BLK)

        @pl.when(j == 6)
        def _():
            send_p(False, 2, BLK)
            send_p(True, 3, 0)

        @pl.when(j == 7)
        def _():
            acc_p[...] = part[0:BLK, :]
            acc_q[...] = part[BLK : 2 * BLK, :]

        return carry

    lax.fori_loop(0, 8, second, 0)

    def late(i, carry):
        off1, off2 = chunk(i)
        keys = jnp.concatenate([kvb[pl.ds(off1, 256), 0:D], kvb[pl.ds(off2, 256), 0:D]], axis=0)
        dqt[...] += dot(keys, dss[pl.ds(pl.multiple_of(i * 512, 512), 512), :], TN)

        @pl.when(i == 1)
        def _():
            total = acc_q[...]
            for k in range(1, NU):
                t_qu(k).wait_recv()
                total = total + rq_in[k].astype(F32)
            acc_q[...] = total
            sz_out[...] = total.astype(BF)
            for k in (4, 3, 5, 2, 6, 1, 7):
                t_qz(k).start()

        @pl.when(i == 2)
        def _():
            total = acc_p[...]
            for k in range(SUMS):
                t_pz(True, 3, k).wait_recv()
                t_pz(False, 2, k).wait_recv()
            total = total + r_r[3].astype(F32) + r_l[2].astype(F32)
            acc_p[...] = total
            sp_out[...] = total.astype(BF)
            for k in range(1, NU):
                t_pu(k).start()

        return carry

    lax.fori_loop(0, 8, late, 0)

    own_w = eo[...] * zs[0:1, ROWS : 2 * ROWS]
    kvg[3] = dot(own_w.astype(BF), dos[ROWS : 2 * ROWS], NN)
    own_g = dot(rv[...], dos[ROWS : 2 * ROWS], NT) - dvec[0:1, ROWS : 2 * ROWS]
    own_g = (own_w * own_g).astype(BF)
    kvg[2] = dot(own_g, qs[ROWS : 2 * ROWS], NN) * SCALE
    dqt[:, ROWS : 2 * ROWS] += dot(rk[...], own_g, TN)

    stores = [
        pltpu.make_async_copy(dq.at[0], dq_hbm.at[0], osem.at[0]),
        pltpu.make_async_copy(dq.at[1], dq_hbm.at[1], osem.at[1]),
        pltpu.make_async_copy(kvg, kvg_hbm, osem.at[2]),
    ]
    for which, first_col in ((0, 0), (1, ROWS)):
        for h in range(0, H, 2):
            block = dqt[:, first_col + h * R : first_col + (h + 2) * R].T * SCALE
            dq[which, :, h * D : (h + 1) * D] = block[0:R]
            dq[which, :, (h + 1) * D : (h + 2) * D] = block[R : 2 * R]
        stores[which].start()

    for i in range(1, NU):
        t_qz(i).wait_recv()
        t_pu(i).wait_recv()
    for acc, arrivals, place, first_row in ((acc_p, rp_in, u, 0), (acc_q, rz_in, z, S)):
        total = acc[pl.ds(pl.multiple_of(place * S, S), S), :]
        for i in range(1, NU):
            total = total + arrivals[i].astype(F32)
        kvg[0, first_row : first_row + S, :] = total[:, 0:D] * SCALE
        kvg[1, first_row : first_row + S, :] = total[:, D : 2 * D]
    stores[2].start()

    for i in range(1, NU):
        for sent in (g_pu, g_qz, g_qu, t_qu, t_pu, t_qz):
            sent(i).wait_send()
    for i in range(1, 4):
        g_v(i).wait_send()
    for right in (True, False):
        for s in range(NZ // 2):
            for k in pieces(right, s):
                g_pz(right, s, k).wait_send()
            if right or s < 3:
                for k in range(SUMS):
                    t_pz(right, s, k).wait_send()
    for store in stores:
        store.wait()


def hand_out(dq, kvg, pdq, pdk, pdv, rdq, rdk, rdv):
    pdq[...] = dq[0]
    rdq[...] = dq[1]
    for i, out in enumerate((pdk, pdv, rdk, rdv)):
        out[...] = kvg[i]


def local(
    prompt_q, prompt_k, prompt_v, prompt_out, prompt_dout,
    resp_q, resp_k, resp_v, resp_out, resp_dout, resp_len, loss_mask,
):
    vmem = pl.BlockSpec(memory_space=pltpu.VMEM)
    anywhere = pl.BlockSpec(memory_space=pl.ANY)
    wide_out = jax.ShapeDtypeStruct((R, H * D), F32)
    head_out = jax.ShapeDtypeStruct((R, D), F32)
    V = pltpu.VMEM
    head_in = V((R, D), BF)
    sums = pl.pallas_call(
        kernel,
        out_shape=[jax.ShapeDtypeStruct((2, R, H * D), F32), jax.ShapeDtypeStruct((4, R, D), F32)],
        in_specs=[anywhere] * 10 + [vmem] * 2,
        out_specs=[anywhere] * 2,
        scratch_shapes=[
            head_in, head_in, head_in, head_in, V((16, 4 * H * D), BF),
            V((2, R, H * D), F32),
            V((4, R, D), F32),
            V((2 * HALF, 2 * D), BF),
            V((2 * ROWS, D), BF),
            V((2 * ROWS, D), BF),
            V((2 * HALF, 2 * ROWS), F32),
            V((R, ROWS), F32),
            V((2 * HALF, 2 * ROWS), BF),
            V((8, 2 * ROWS), F32),
            V((8, 2 * ROWS), F32),
            V((D, 2 * ROWS), F32),
            V((512, 2 * D), F32),
            V((BLK, 2 * D), F32),
            V((BLK, 2 * D), F32),
            V((4, BLK, 2 * D), BF),
            V((3, BLK, 2 * D), BF),
            V((4, BLK, 2 * D), BF),
            V((3, BLK, 2 * D), BF),
            V((NU, BLK, 2 * D), BF),
            V((NU, BLK, 2 * D), BF),
            V((BLK, 2 * D), BF),
            V((NU, S, 2 * D), BF),
            V((BLK, 2 * D), BF),
            V((NZ, S, 2 * D), BF),
            pltpu.SemaphoreType.DMA((COPIES,)),
            pltpu.SemaphoreType.DMA((COPIES,)),
            pltpu.SemaphoreType.DMA((10,)),
            pltpu.SemaphoreType.DMA((3,)),
        ],
        compiler_params=pltpu.CompilerParams(
            collective_id=0, has_side_effects=True, vmem_limit_bytes=127 * 2**19
        ),
    )(
        prompt_q, prompt_k, prompt_v, prompt_out, prompt_dout,
        resp_q, resp_k, resp_v, resp_out, resp_dout, resp_len.reshape(1, 1), loss_mask.reshape(1, R),
    )
    return pl.pallas_call(
        hand_out,
        out_shape=[wide_out, head_out, head_out, wide_out, head_out, head_out],
        in_specs=[vmem] * 2,
        out_specs=[vmem] * 6,
    )(*sums)


def solution(mesh):
    grid = P("wide", "kv")
    return jax.shard_map(
        local,
        mesh=mesh,
        in_specs=(grid,) * 9 + (P(("wide", "kv"), None), P("wide"), P("wide")),
        out_specs=(grid,) * 6,
        check_vma=False,
    )
```

```python
import functools
import math

import jax
import jax.numpy as jnp
from jax import lax
from jax.experimental import pallas as pl
from jax.experimental.pallas import tpu as pltpu
from jax.sharding import PartitionSpec as P

MESH = pl.DeviceIdType.MESH
BF = jnp.bfloat16
F32 = jnp.float32
NX, NZ, NY = 4, 8, 2
NU = NX * NY
R = 64
S = R // 2
D = 128
H = 16
ROWS = H * R
SCALE = 1.0 / math.sqrt(D)
EXP2_SCALE = math.log2(math.e) / math.sqrt(D)
HALF = NU * NZ * S
BLK = NU * S
SUBS = NX
PIECE = BLK // SUBS
SUMS = 2
SUM_PIECE = BLK // SUMS
NN = (((1,), (0,)), ((), ()))
NT = (((1,), (1,)), ((), ()))
TN = (((0,), (0,)), ((), ()))
COPIES = 69


def dot(a, b, dims):
    return lax.dot_general(a, b, dims, preferred_element_type=F32)


def by_head(ref):
    return jnp.concatenate([ref[:, h * D : (h + 1) * D] for h in range(H)], axis=0)


def lane_dots(a, b):
    prod = a.astype(F32) * b.astype(F32)
    high = prod.astype(BF)
    low = (prod - high.astype(F32)).astype(BF)
    ones = jnp.ones((8, D), BF)
    return dot(ones, high, NT) + dot(ones, low, NT)


def kernel(
    pq_hbm, pk_hbm, pv_hbm, po_hbm, pdo_hbm, rq_hbm, rk_hbm, rv_hbm, ro_hbm, rdo_hbm, rlen, lmask,
    dq_hbm, kvg_hbm,
    pk, pv, rk, rv, rdo, dq, kvg,
    kvb, qs, dos, e, eo, dss, zs, dvec, dqt, part, acc_p, acc_q,
    s_r, s_l, r_r, r_l, sq, rq_in, sp_out, rp_in, sz_out, rz_in,
    ssem, rsem, lsem, osem,
):
    w, kv = lax.axis_index("wide"), lax.axis_index("kv")
    x, z, y = w // (NZ * NY), lax.rem(w // NY, NZ), lax.rem(w, NY)
    u = x * NY + y

    def dev(uu, zz, vv):
        return (((uu // NY) * NZ + zz) * NY + lax.rem(uu, NY), vv)

    def u_to(i):
        return lax.rem(x + i // NY, NX) * NY + lax.rem(y + lax.rem(i, NY), NY)

    def u_from(i):
        return lax.rem(x + NX - i // NY, NX) * NY + lax.rem(y + lax.rem(i, NY), NY)

    def up(i):
        return dev(u_to(i), z, kv)

    def zp(i):
        return dev(u, lax.rem(z + i, NZ), kv)

    def vp(i):
        return dev(u, z, lax.rem(kv + i, 4))

    barrier = pltpu.get_barrier_semaphore()
    peers = [zp(i) for i in range(1, NZ)] + [up(i) for i in range(1, NU)] + [vp(i) for i in range(1, 4)]
    for peer in peers:
        pl.semaphore_signal(barrier, inc=1, device_id=peer, device_id_type=MESH)

    pq, po, pdo, rq, ro, arrived = (dss.at[pl.ds(i * R, R)] for i in range(6))
    hbm = (pk_hbm, pv_hbm, rq_hbm, rk_hbm, pq_hbm, pdo_hbm, po_hbm, rdo_hbm, ro_hbm, rv_hbm)
    loads = [
        pltpu.make_async_copy(src, dst, lsem.at[i])
        for i, (src, dst) in enumerate(zip(hbm, (pk, pv, rq, rk, pq, pdo, po, rdo, ro, rv), strict=True))
    ]
    for load in loads:
        load.start()

    sem_no = {}

    def copy(key, src, dst, to):
        if key[0] in ("gqz", "tpu", "tqz"):
            key = key[0]
        i = sem_no.setdefault(key, len(sem_no))
        return pltpu.make_async_remote_copy(
            src_ref=src, dst_ref=dst, send_sem=ssem.at[i], recv_sem=rsem.at[i],
            device_id=to, device_id_type=MESH,
        )

    def seven(key, ref):
        return copy((key,), ref, ref, zp(1))

    def g_qz_all():
        return seven("gqz", kvb.at[pl.ds(0, (NZ - 1) * S)])

    def t_pu_all():
        return seven("tpu", rp_in.at[pl.ds(1, NU - 1)])

    def t_qz_all():
        return seven("tqz", rz_in.at[pl.ds(1, NZ - 1)])

    def rows(off, n):
        return kvb.at[pl.ds(pl.multiple_of(off, S), n)]

    own_p = z * BLK + u * S
    own_q = HALF + u * BLK + z * S

    def g_pu(i):
        return copy(("gpu", i), rows(own_p, S), rows(own_p, S), up(i))

    def g_qz(i):
        return copy(("gqz", i), rows(own_q, S), rows(own_q, S), zp(i))

    def g_pz(right, s, k):
        at = lax.rem(x + NX - k, NX)
        b = rows(lax.rem(z + (NZ - s if right else s), NZ) * BLK + at * PIECE, PIECE)
        return copy(("gpz", right, s, k), b, b, zp(1 if right else NZ - 1))

    def g_qu(i):
        return copy(("gqu", i), rows(HALF + u * BLK, BLK), rows(HALF + u * BLK, BLK), up(i))

    def g_v(i):
        col = pl.multiple_of(lax.rem(kv + i, 4) * (H * D), H * D)
        return copy(
            ("gv", i),
            rdo.at[:, pl.ds(col, H * D)],
            arrived.at[pl.ds(pl.multiple_of(kv * 16, 16), 16)],
            vp(i),
        )

    def pieces(right, s):
        if s < NZ // 2 - 1:
            return range(SUBS)
        return range(SUBS // 2) if right else range(SUBS // 2, SUBS)

    def t_pz(right, t, k):
        part_of = pl.ds(k * SUM_PIECE, SUM_PIECE)
        if right:
            return copy(("tpr", t, k), s_r.at[t, part_of], r_r.at[t, part_of], zp(1))
        return copy(("tpl", t, k), s_l.at[t, part_of], r_l.at[t, part_of], zp(NZ - 1))

    def t_qu(i):
        return copy(("tqu", i), sq.at[i], rq_in.at[i], up(i))

    def t_pu(i):
        src = sp_out.at[pl.ds(pl.multiple_of(u_to(i) * S, S), S)]
        return copy(("tpu", i), src, rp_in.at[i], up(i))

    def t_qz(i):
        src = sz_out.at[pl.ds(pl.multiple_of(lax.rem(z + i, NZ) * S, S), S)]
        return copy(("tqz", i), src, rz_in.at[i], zp(i))

    for load in loads:
        load.wait()
    for off, first_row in ((own_p, 0), (own_q, S)):
        kvb[pl.ds(pl.multiple_of(off, S), S), 0:D] = pk[first_row : first_row + S, :]
        kvb[pl.ds(pl.multiple_of(off, S), S), D : 2 * D] = pv[first_row : first_row + S, :]
    qs[0:ROWS] = by_head(pq)
    qs[ROWS : 2 * ROWS] = by_head(rq)
    prompt_cot = by_head(pdo)
    dos[0:ROWS] = prompt_cot
    dvec[:, 0:ROWS] = lane_dots(prompt_cot, by_head(po))
    dqt[...] = jnp.zeros_like(dqt)
    row_minus_col = lax.broadcasted_iota(jnp.int32, (R, ROWS), 0) - lax.rem(
        lax.broadcasted_iota(jnp.int32, (R, ROWS), 1), R
    )
    own_e = jnp.where(
        row_minus_col <= 0, jnp.exp2(dot(rk[...], qs[ROWS : 2 * ROWS], NT) * EXP2_SCALE), 0.0
    )
    eo[...] = own_e
    zs[:, 0:ROWS] = jnp.zeros((8, ROWS), F32)
    zs[:, ROWS : 2 * ROWS] = jnp.sum(own_e.reshape(R // 8, 8, ROWS), axis=0)
    pl.semaphore_wait(barrier, len(peers))

    for i in range(1, NU):
        g_pu(i).start()
    for i in (4, 3, 5, 2, 6, 1, 7):
        g_qz(i).start()
    for i in range(1, 4):
        g_v(i).start()
    arrived[pl.ds(pl.multiple_of(kv * 16, 16), 16), :] = rdo[:, pl.ds(pl.multiple_of(kv * (H * D), H * D), H * D)]
    for k in range(SUBS):
        for i in range(NY * k, NY * (k + 1)):
            if i > 0:
                g_pu(i).wait_recv()
        g_pz(True, 0, k).start()
        g_pz(False, 0, k).start()
    g_qz_all().wait_recv()
    for i in range(1, NU):
        g_qu(i).start()

    def response_cotangents():
        for i in range(1, 4):
            g_v(i).wait_recv()
        tokens = lax.broadcasted_iota(jnp.int32, (R, R), 1)
        usable = (lmask[...] == 1) & (lax.broadcasted_iota(jnp.int32, (1, R), 1) < rlen[...])
        diagonal = lax.broadcasted_iota(jnp.int32, (R, R), 0) == tokens
        keep = jnp.sum(jnp.where(diagonal & usable, 1.0, 0.0), axis=1, keepdims=True)
        keep = jnp.broadcast_to(keep, (R, D)) > 0.5
        keep = jnp.concatenate([keep] * H, axis=0)
        cot = jnp.where(keep, by_head(arrived).astype(F32), 0.0).astype(BF)
        dos[ROWS : 2 * ROWS] = cot
        dvec[:, ROWS : 2 * ROWS] = lane_dots(cot, by_head(ro))

    def first(j, carry):
        for s in range(NZ // 2):

            @pl.when(j == (s + 1 if s < NZ // 2 - 1 else 7))
            def _():
                for k in range(SUBS):
                    for right in (True, False):
                        if k in pieces(right, s):
                            g_pz(right, s, k).wait_recv()
                            if s < NZ // 2 - 1 and k in pieces(right, s + 1):
                                g_pz(right, s + 1, k).start()
                if s == NZ // 2 - 1:
                    g_qu(NU - 1).wait_recv()

        @pl.when(j == NU // 2)
        def _():
            response_cotangents()

        for c in range(1, NU // 2):

            @pl.when(j == NU // 2 - 1 + c)
            def _():
                g_qu(2 * c - 1).wait_recv()
                g_qu(2 * c).wait_recv()

        q, opening, closing = j // 4, 1 - (j + 7) // 8, j // 7
        p1, p2 = 1 - q + closing, (1 - q) * (1 - opening)
        z1 = lax.rem(z + NZ - j * (1 - q) - 4 * closing, NZ)
        z2 = lax.rem(z + j, NZ)
        u1 = u_from(lax.rem(2 * NU + 2 * j - 7, NU))
        u2 = u_from(q * (2 * j - 6) - closing)
        off1 = p1 * (z1 * BLK) + (1 - p1) * (HALF + u1 * BLK)
        off2 = p2 * (z2 * BLK) + (1 - p2) * (HALF + u2 * BLK)
        off1, off2 = pl.multiple_of(off1, BLK), pl.multiple_of(off2, BLK)
        keys = jnp.concatenate([kvb[pl.ds(off1, 256), 0:D], kvb[pl.ds(off2, 256), 0:D]], axis=0)
        ex = jnp.exp2(dot(keys, qs[...], NT) * EXP2_SCALE)
        seen = []
        for p, zz, uu, top in ((p1, z1, u1, 0), (p2, z2, u2, BLK)):
            for g in range(8):
                in_p = (g // NY) * (NZ * NY) + zz * NY + g % NY
                in_q = (uu // NY) * (NZ * NY) + g * NY + lax.rem(uu, NY)
                limit = (w - (p * in_p + (1 - p) * in_q)) * R - (1 - p) * S
                block = ex[top + g * S : top + (g + 1) * S, 0:ROWS]
                seen.append(jnp.where(row_minus_col[0:S] <= limit, block, 0.0))
        seen = jnp.concatenate(seen, axis=0)
        rest = ex[:, ROWS : 2 * ROWS]
        for k, off in ((0, off1), (1, off2)):
            e[pl.ds(off, 256), 0:ROWS] = seen[k * 256 : (k + 1) * 256]
            e[pl.ds(off, 256), ROWS : 2 * ROWS] = rest[k * 256 : (k + 1) * 256]
        zs[:, 0:ROWS] += jnp.sum(seen.reshape(64, 8, ROWS), axis=0)
        zs[:, ROWS : 2 * ROWS] += jnp.sum(rest.reshape(64, 8, ROWS), axis=0)
        return carry

    lax.fori_loop(0, 8, first, 0)

    zs[...] = jnp.broadcast_to(1.0 / jnp.sum(zs[...], axis=0, keepdims=True), zs.shape)

    def chunk(j):
        odd, from_5, from_6, last = lax.rem(j, 2), j // 5, j // 6, j // 7
        p1 = 1 - odd + last
        p2 = (1 - odd) * (1 - (j // 4) * (1 - from_5))
        z1, z2 = lax.rem(z + 4 - j // 2 - last, NZ), lax.rem(z + 5 + j // 2 - from_6, NZ)
        u1, u2 = u_to(8 - j - from_5), u_to(7 - j - from_5 + last)
        off1 = p1 * (z1 * BLK) + (1 - p1) * (HALF + u1 * BLK)
        off2 = p2 * (z2 * BLK) + (1 - p2) * (HALF + u2 * BLK)
        return pl.multiple_of(off1, BLK), pl.multiple_of(off2, BLK)

    def second(j, carry):
        off1, off2 = chunk(j)
        for off, top in ((off1, 0), (off2, BLK)):
            weights = e[pl.ds(off, BLK), :] * zs[0:1, :]
            part[top : top + BLK, D : 2 * D] = dot(weights.astype(BF), dos[...], NN)
            weight_grad = dot(kvb[pl.ds(off, BLK), D : 2 * D], dos[...], NT)
            score_grad = (weights * (weight_grad - dvec[0:1, :])).astype(BF)
            dss[pl.ds(pl.multiple_of(j * (2 * BLK), 2 * BLK) + top, BLK), :] = score_grad
            part[top : top + BLK, 0:D] = dot(score_grad, qs[...], NN)

        def send_p(right, t, top):
            sent, arrived_sum = (s_r, r_r) if right else (s_l, r_l)
            for k in range(SUMS):
                piece = pl.ds(k * SUM_PIECE, SUM_PIECE)
                value = part[top + k * SUM_PIECE : top + (k + 1) * SUM_PIECE, :]
                if t > 0:
                    t_pz(right, t - 1, k).wait_recv()
                    value = value + arrived_sum[t - 1, piece].astype(F32)
                sent[t, piece] = value.astype(BF)
                t_pz(right, t, k).start()

        def send_q(i, top):
            sq[i] = part[top : top + BLK, :].astype(BF)
            t_qu(i).start()

        @pl.when(j == 0)
        def _():
            send_p(True, 0, 0)
            send_p(False, 0, BLK)

        @pl.when(j == 1)
        def _():
            send_q(7, 0)
            send_q(6, BLK)

        @pl.when(j == 2)
        def _():
            send_p(True, 1, 0)
            send_p(False, 1, BLK)

        @pl.when(j == 3)
        def _():
            send_q(5, 0)
            send_q(4, BLK)

        @pl.when(j == 4)
        def _():
            send_q(3, BLK)
            send_p(True, 2, 0)

        @pl.when(j == 5)
        def _():
            send_q(2, 0)
            send_q(1, BLK)

        @pl.when(j == 6)
        def _():
            send_p(False, 2, BLK)
            send_p(True, 3, 0)

        @pl.when(j == 7)
        def _():
            acc_p[...] = part[0:BLK, :]
            acc_q[...] = part[BLK : 2 * BLK, :]

        return carry

    lax.fori_loop(0, 8, second, 0)

    def late(i, carry):
        off1, off2 = chunk(i)
        keys = jnp.concatenate([kvb[pl.ds(off1, 256), 0:D], kvb[pl.ds(off2, 256), 0:D]], axis=0)
        dqt[...] += dot(keys, dss[pl.ds(pl.multiple_of(i * 512, 512), 512), :], TN)

        @pl.when(i == 1)
        def _():
            total = acc_q[...]
            for k in range(1, NU):
                t_qu(k).wait_recv()
                total = total + rq_in[k].astype(F32)
            acc_q[...] = total
            sz_out[...] = total.astype(BF)
            for k in (4, 3, 5, 2, 6, 1, 7):
                t_qz(k).start()

        @pl.when(i == 2)
        def _():
            total = acc_p[...]
            for k in range(SUMS):
                t_pz(True, 3, k).wait_recv()
                t_pz(False, 2, k).wait_recv()
            total = total + r_r[3].astype(F32) + r_l[2].astype(F32)
            acc_p[...] = total
            sp_out[...] = total.astype(BF)
            for k in range(1, NU):
                t_pu(k).start()

        return carry

    lax.fori_loop(0, 8, late, 0)

    own_w = eo[...] * zs[0:1, ROWS : 2 * ROWS]
    kvg[3] = dot(own_w.astype(BF), dos[ROWS : 2 * ROWS], NN)
    own_g = dot(rv[...], dos[ROWS : 2 * ROWS], NT) - dvec[0:1, ROWS : 2 * ROWS]
    own_g = (own_w * own_g).astype(BF)
    kvg[2] = dot(own_g, qs[ROWS : 2 * ROWS], NN) * SCALE
    dqt[:, ROWS : 2 * ROWS] += dot(rk[...], own_g, TN)

    stores = [
        pltpu.make_async_copy(dq.at[0], dq_hbm.at[0], osem.at[0]),
        pltpu.make_async_copy(dq.at[1], dq_hbm.at[1], osem.at[1]),
        pltpu.make_async_copy(kvg, kvg_hbm, osem.at[2]),
    ]
    for which, first_col in ((0, 0), (1, ROWS)):
        for h in range(0, H, 2):
            block = dqt[:, first_col + h * R : first_col + (h + 2) * R].T * SCALE
            dq[which, :, h * D : (h + 1) * D] = block[0:R]
            dq[which, :, (h + 1) * D : (h + 2) * D] = block[R : 2 * R]
        stores[which].start()

    t_qz_all().wait_recv()
    t_pu_all().wait_recv()
    for acc, arrivals, place, first_row in ((acc_p, rp_in, u, 0), (acc_q, rz_in, z, S)):
        total = acc[pl.ds(pl.multiple_of(place * S, S), S), :]
        for i in range(1, NU):
            total = total + arrivals[i].astype(F32)
        kvg[0, first_row : first_row + S, :] = total[:, 0:D] * SCALE
        kvg[1, first_row : first_row + S, :] = total[:, D : 2 * D]
    stores[2].start()

    for i in range(1, NU):
        for sent in (g_pu, g_qu, t_qu):
            sent(i).wait_send()
    for every in (g_qz_all, t_pu_all, t_qz_all):
        every().wait_send()
    for i in range(1, 4):
        g_v(i).wait_send()
    for right in (True, False):
        for s in range(NZ // 2):
            for k in pieces(right, s):
                g_pz(right, s, k).wait_send()
            if right or s < 3:
                for k in range(SUMS):
                    t_pz(right, s, k).wait_send()
    for store in stores:
        store.wait()


def hand_out(dq_hbm, kvg_hbm, pdq, pdk, pdv, rdq, rdk, rdv, dq, kvg, isem, osem):
    loads = [
        pltpu.make_async_copy(dq_hbm.at[0], dq.at[0], isem.at[0]),
        pltpu.make_async_copy(dq_hbm.at[1], dq.at[1], isem.at[1]),
        pltpu.make_async_copy(kvg_hbm, kvg, isem.at[2]),
    ]
    for load in loads:
        load.start()
    stores = [pltpu.make_async_copy(dq.at[i], out, osem.at[i]) for i, out in enumerate((pdq, rdq))]
    stores += [pltpu.make_async_copy(kvg.at[i], out, osem.at[2 + i]) for i, out in enumerate((pdk, pdv, rdk, rdv))]
    loads[0].wait()
    stores[0].start()
    loads[1].wait()
    stores[1].start()
    loads[2].wait()
    for store in stores[2:]:
        store.start()
    for store in stores:
        store.wait()


def local(
    prompt_q, prompt_k, prompt_v, prompt_out, prompt_dout,
    resp_q, resp_k, resp_v, resp_out, resp_dout, resp_len, loss_mask,
):
    vmem = pl.BlockSpec(memory_space=pltpu.VMEM)
    anywhere = pl.BlockSpec(memory_space=pl.ANY)
    wide_out = jax.ShapeDtypeStruct((R, H * D), F32)
    head_out = jax.ShapeDtypeStruct((R, D), F32)
    V = pltpu.VMEM
    head_in = V((R, D), BF)
    sums = pl.pallas_call(
        kernel,
        out_shape=[jax.ShapeDtypeStruct((2, R, H * D), F32), jax.ShapeDtypeStruct((4, R, D), F32)],
        in_specs=[anywhere] * 10 + [vmem] * 2,
        out_specs=[anywhere] * 2,
        scratch_shapes=[
            head_in, head_in, head_in, head_in, V((16, 4 * H * D), BF),
            V((2, R, H * D), F32),
            V((4, R, D), F32),
            V((2 * HALF, 2 * D), BF),
            V((2 * ROWS, D), BF),
            V((2 * ROWS, D), BF),
            V((2 * HALF, 2 * ROWS), F32),
            V((R, ROWS), F32),
            V((2 * HALF, 2 * ROWS), BF),
            V((8, 2 * ROWS), F32),
            V((8, 2 * ROWS), F32),
            V((D, 2 * ROWS), F32),
            V((512, 2 * D), F32),
            V((BLK, 2 * D), F32),
            V((BLK, 2 * D), F32),
            V((4, BLK, 2 * D), BF),
            V((3, BLK, 2 * D), BF),
            V((4, BLK, 2 * D), BF),
            V((3, BLK, 2 * D), BF),
            V((NU, BLK, 2 * D), BF),
            V((NU, BLK, 2 * D), BF),
            V((BLK, 2 * D), BF),
            V((NU, S, 2 * D), BF),
            V((BLK, 2 * D), BF),
            V((NZ, S, 2 * D), BF),
            pltpu.SemaphoreType.DMA((COPIES,)),
            pltpu.SemaphoreType.DMA((COPIES,)),
            pltpu.SemaphoreType.DMA((10,)),
            pltpu.SemaphoreType.DMA((3,)),
        ],
        compiler_params=pltpu.CompilerParams(
            collective_id=0, has_side_effects=True, vmem_limit_bytes=127 * 2**19
        ),
    )(
        prompt_q, prompt_k, prompt_v, prompt_out, prompt_dout,
        resp_q, resp_k, resp_v, resp_out, resp_dout, resp_len.reshape(1, 1), loss_mask.reshape(1, R),
    )
    return pl.pallas_call(
        hand_out,
        out_shape=[wide_out, head_out, head_out, wide_out, head_out, head_out],
        in_specs=[anywhere] * 2,
        out_specs=[anywhere] * 6,
        scratch_shapes=[
            V((2, R, H * D), F32),
            V((4, R, D), F32),
            pltpu.SemaphoreType.DMA((3,)),
            pltpu.SemaphoreType.DMA((6,)),
        ],
    )(*sums)


def solution(mesh):
    grid = P("wide", "kv")
    return jax.shard_map(
        local,
        mesh=mesh,
        in_specs=(grid,) * 9 + (P(("wide", "kv"), None), P("wide"), P("wide")),
        out_specs=(grid,) * 6,
        check_vma=False,
    )
```
